32 devices in a mesh: fsdp: 8 (over y, x, core), tp: 4 (over z).
Axes of the slice: x: 2, y: 2, z: 4, core: 2. Of those that a mesh axis runs over, the one named last changes fastest.
Arguments:
- tokens: bfloat16 [16, 1024, 2048], P('fsdp', 'tp'), may hold values from -6 to 6
- lengths: int32 [16], P('fsdp'), may hold values from 256 to 1024, as said below
- routes: int32 [16, 1024, 6], P('fsdp'), may hold values from 0 to 7, as said below
- slot_ranks: int32 [16, 1024, 6], P('fsdp'), may hold values from 0 to 1024, as said below
- attn_gain: bfloat16 [2048], P('fsdp'), may hold values from 0.099609375 to 1.8984375
- query_weight: bfloat16 [2048, 3072], P('fsdp', 'tp'), may hold values from -0.125 to 0.125
- latent_key_weight: bfloat16 [2048, 576], P('fsdp'), may hold values from -0.125 to 0.125
- latent_gain: bfloat16 [512], P('fsdp'), may hold values from 0.099609375 to 1.8984375
- kvb_weight: bfloat16 [512, 4096], P('fsdp', 'tp'), may hold values from -0.25 to 0.25
- output_weight: bfloat16 [2048, 2048], P('tp', 'fsdp'), may hold values from -2 to 2
- ffn_gain: bfloat16 [2048], P('fsdp'), may hold values from 0.099609375 to 1.8984375
- router_matrix: bfloat16 [2048, 8], P('fsdp'), may hold values from -0.0625 to 0.0625
- shared_gate_weight: bfloat16 [2048, 2816], P('fsdp', 'tp'), may hold values from -0.125 to 0.125
- shared_up_weight: bfloat16 [2048, 2816], P('fsdp', 'tp'), may hold values from -0.125 to 0.125
- shared_down_weight: bfloat16 [2816, 2048], P('tp', 'fsdp'), may hold values from -0.109375 to 0.109375
- expert_gate: bfloat16 [8, 2048, 1408], P('fsdp', None, 'tp'), may hold values from -0.125 to 0.125
- expert_up: bfloat16 [8, 2048, 1408], P('fsdp', None, 'tp'), may hold values from -0.125 to 0.125
- expert_down: bfloat16 [8, 1408, 2048], P('fsdp', 'tp'), may hold values from -0.15625 to 0.15625
- cotangent: bfloat16 [16, 1024, 2048], P('fsdp', 'tp'), may hold values from -6 to 6
Outputs:
- output: bfloat16 [16, 1024, 2048], P('fsdp', 'tp')
- grad_tokens: bfloat16 [16, 1024, 2048], P('fsdp', 'tp')
- grad_attn_gain: float32 [2048], P('fsdp')
- grad_q_weight: float32 [2048, 3072], P('fsdp', 'tp')
- grad_kva_weight: float32 [2048, 576], P('fsdp')
- grad_latent_gain: float32 [512], P('fsdp')
- grad_kvb_weight: float32 [512, 4096], P('fsdp', 'tp')
- grad_out_weight: float32 [2048, 2048], P('tp', 'fsdp')
- grad_ffn_gain: float32 [2048], P('fsdp')
- grad_router_weight: float32 [2048, 8], P('fsdp')
- grad_shared_gate: float32 [2048, 2816], P('fsdp', 'tp')
- grad_shared_up: float32 [2048, 2816], P('fsdp', 'tp')
- grad_shared_down: float32 [2816, 2048], P('tp', 'fsdp')
- grad_expert_gate: float32 [8, 2048, 1408], P('fsdp', None, 'tp')
- grad_expert_up: float32 [8, 2048, 1408], P('fsdp', None, 'tp')
- grad_expert_down: float32 [8, 1408, 2048], P('fsdp', 'tp')
The draws below stay inside these ranges and needn't reach their ends.
Inputs may be any that keep to these rules, and one draw needn't show every extreme that they name: `lengths`: of each 2 consecutive sequences one, which one varies, has length 1024; the others have 1024 // 4 or more. `routes`: the 6 experts of a token are different. For a token below its sequence's length, slot_ranks[s, t, k] is the rank of that route among the routes to the same expert from the same 2 consecutive sequences, taken in order of sequence, position and k and counting only tokens below their lengths, where that rank is below 1024; it is 1024 otherwise and for every token at or beyond its length. In every block of 2 sequences some expert gets more than 1024 such routes.
All inputs are finite; a program needn't handle non-finite values.
Results may differ from the reference program's by a relative error of at most 0.034.
Values may be sent and summed in bfloat16 or wider, within the bound.
A program may use at most 576 MiB of HBM per device.

```python
from functools import partial
import jax
import jax.numpy as jnp
from jax import lax

D = 2048
HEAD_COUNT = 16
PLAIN_WIDTH = 128
ROTARY_WIDTH = 64
VALUE_WIDTH = 128
RANK = 512
FFE = 1408
SFF = 2816
TOPK = 6
SEQUENCE_LENGTH = 1024
SEQ_G = 2
EXPERTS = 8
SEQUENCE_COUNT = 16
CAP = 1024


def route_table(key):
    group_count = SEQUENCE_COUNT // SEQ_G
    group_rows = SEQ_G * SEQUENCE_LENGTH
    key_full, key_len, key_pop, key_hot, key_noise = jax.random.split(key, 5)
    full_index = jax.random.randint(key_full, (group_count, 1), 0, SEQ_G)
    drawn_lengths = jax.random.randint(key_len, (group_count, SEQ_G), SEQUENCE_LENGTH // 4, SEQUENCE_LENGTH + 1)
    lengths = jnp.where(jnp.arange(SEQ_G)[None, :] == full_index, SEQUENCE_LENGTH, drawn_lengths).astype(jnp.int32)
    expert_ids = jnp.arange(EXPERTS, dtype=jnp.int32)
    popular = jax.random.randint(key_pop, (group_count, 1, EXPERTS), 0, 1024)
    hot_expert = jax.random.randint(key_hot, (group_count, 1, 1), 0, EXPERTS)
    boosted = jnp.where(expert_ids[None, None, :] == hot_expert, 4096, 0)
    noise_scores = jax.random.randint(key_noise, (group_count, group_rows, EXPERTS), 0, 1024)
    scores = (noise_scores + popular + boosted) * EXPERTS + expert_ids
    routes = lax.top_k(scores, TOPK)[1].astype(jnp.int32)
    positions = jnp.arange(group_rows, dtype=jnp.int32)
    repeated = jnp.repeat(lengths, SEQUENCE_LENGTH, axis=1)
    valid_mask = (positions % SEQUENCE_LENGTH)[None, :] < repeated
    chosen = ((routes[..., None] == expert_ids) & valid_mask[:, :, None, None]).astype(jnp.int32)
    chosen = chosen.reshape(group_count, group_rows * TOPK, EXPERTS)
    ranks = jnp.cumsum(chosen, axis=1) - chosen
    ranks = jnp.sum(ranks * chosen, axis=-1).reshape(group_count, group_rows, TOPK)
    slot_ranks = jnp.where(valid_mask[:, :, None] & (ranks < CAP), ranks, CAP).astype(jnp.int32)
    return (lengths.reshape(SEQUENCE_COUNT), routes.reshape(SEQUENCE_COUNT, SEQUENCE_LENGTH, TOPK), slot_ranks.reshape(SEQUENCE_COUNT, SEQUENCE_LENGTH, TOPK))


def draw_lengths(key, part):
    return route_table(key)[0]


def draw_routes(key, part):
    return route_table(key)[1]


def draw_slot_ranks(key, part):
    return route_table(key)[2]


def level_of(rng, shape, cuts, low, high):
    gain, own = 1.0, jax.random.fold_in(rng, 6)
    for dim, shards_of in cuts:
        draws = jnp.exp(jax.random.uniform(jax.random.fold_in(own, dim), (shards_of,), jnp.float32, low / len(cuts), high / len(cuts)))
        gain = gain * jnp.repeat(draws, shape[dim] // shards_of).reshape([-1 if axis == dim else 1 for axis in range(len(shape))])
    return gain


def gaussian(key, extent, width, bound, cuts=(), held_as=jnp.bfloat16):
    entries = width * jax.random.normal(key, extent, jnp.float32)
    if cuts:
        entries = entries * level_of(key, extent, cuts, -0.22, 0.18)
    return jnp.clip(entries, -bound, bound).astype(held_as)


def setup_inputs(seed: int = 0) -> dict:
    keys = jax.random.split(jax.random.key(seed), 20)
    tokens = gaussian(keys[0], (SEQUENCE_COUNT, SEQUENCE_LENGTH, D), 1.0, 6.0, ((0, 8), (1, 4)))
    lengths = draw_lengths(jax.random.fold_in(keys[19], 71), 0)
    routes = draw_routes(jax.random.fold_in(keys[19], 71), 0)
    slot_ranks = draw_slot_ranks(jax.random.fold_in(keys[19], 71), 0)
    attn_gain = jnp.clip(1.0 + 0.18 * jax.random.normal(keys[4], (D,), jnp.float32), 0.099609375, 1.8984375).astype(jnp.bfloat16)
    query_weight = gaussian(keys[5], (D, HEAD_COUNT * (PLAIN_WIDTH + ROTARY_WIDTH)), D ** -0.5, 0.125, ((0, 8), (1, 4)))
    latent_key_weight = gaussian(keys[6], (D, RANK + ROTARY_WIDTH), D ** -0.5, 0.125, ((0, 8),))
    latent_gain = jnp.clip(1.0 + 0.18 * jax.random.normal(keys[7], (RANK,), jnp.float32), 0.099609375, 1.8984375).astype(jnp.bfloat16)
    kvb_weight = gaussian(keys[8], (RANK, HEAD_COUNT * (PLAIN_WIDTH + VALUE_WIDTH)), RANK ** -0.5, 0.25, ((0, 8), (1, 4)))
    output_weight = gaussian(keys[9], (HEAD_COUNT * VALUE_WIDTH, D), (4 * HEAD_COUNT * VALUE_WIDTH // SEQUENCE_LENGTH) ** -0.5, 2.0, ((0, 4), (1, 8)))
    ffn_gain = jnp.clip(1.0 + 0.18 * jax.random.normal(keys[10], (D,), jnp.float32), 0.099609375, 1.8984375).astype(jnp.bfloat16)
    router_matrix = gaussian(keys[11], (D, EXPERTS), (4 * D) ** -0.5, 0.0625, ((0, 8),))
    shared_gate_weight = gaussian(keys[12], (D, SFF), D ** -0.5, 0.125, ((0, 8), (1, 4)))
    shared_up_weight = gaussian(keys[13], (D, SFF), D ** -0.5, 0.125, ((0, 8), (1, 4)))
    shared_down_weight = gaussian(keys[14], (SFF, D), SFF ** -0.5, 0.109375, ((0, 4), (1, 8)))
    expert_gate = gaussian(keys[15], (EXPERTS, D, FFE), D ** -0.5, 0.125, ((0, 8), (2, 4)))
    expert_up = gaussian(keys[16], (EXPERTS, D, FFE), D ** -0.5, 0.125, ((0, 8), (2, 4)))
    expert_down = gaussian(keys[17], (EXPERTS, FFE, D), FFE ** -0.5, 0.15625, ((0, 8), (1, 4)))
    cotangent = gaussian(keys[18], (SEQUENCE_COUNT, SEQUENCE_LENGTH, D), 1.0, 6.0, ((0, 8), (1, 4)))
    return dict(tokens=tokens, lengths=lengths, routes=routes, slot_ranks=slot_ranks, attn_gain=attn_gain, query_weight=query_weight, latent_key_weight=latent_key_weight, latent_gain=latent_gain, kvb_weight=kvb_weight, output_weight=output_weight, ffn_gain=ffn_gain, router_matrix=router_matrix, shared_gate_weight=shared_gate_weight, shared_up_weight=shared_up_weight, shared_down_weight=shared_down_weight, expert_gate=expert_gate, expert_up=expert_up, expert_down=expert_down, cotangent=cotangent)


epsilon = 1e-06
precision_highest = lax.Precision.HIGHEST

@jax.custom_vjp
def low(v):
    return lax.optimization_barrier(v.astype(jnp.bfloat16)).astype(jnp.float32)

@jax.custom_vjp
def lower_backward(v):
    return v

def low_keep(v):
    return (low(v), None)

def low_pass(kept, grad):
    return (grad,)

def back_keep(v):
    return (v, None)

def back_low(kept, grad):
    return (low(grad),)
low.defvjp(low_keep, low_pass)
lower_backward.defvjp(back_keep, back_low)

def normalize(values, gain_row):
    return values * lax.rsqrt(lax.optimization_barrier(jnp.mean(values * values, axis=-1, keepdims=True)) + epsilon) * gain_row

def rotate(values, positions, direction):
    half_width = values.shape[-1] // 2
    frequency = 10000.0 ** (-jnp.arange(half_width, dtype=jnp.float32) / half_width)
    angles = positions.astype(jnp.float32)[..., None] * frequency
    cosines = jnp.cos(angles)
    sines = jnp.sin(angles) * direction
    first_half = values[..., :half_width]
    second_half = values[..., half_width:]
    return jnp.concatenate([first_half * cosines - second_half * sines, first_half * sines + second_half * cosines], axis=-1)

def attend_one(pieces):
    query_nope, query_rope, key_nope, key_rope, values, length_now = pieces
    score_scale = (PLAIN_WIDTH + ROTARY_WIDTH) ** (-0.5)
    scores = jnp.einsum('qhd,khd->hqk', query_nope, key_nope, precision=precision_highest)
    scores = (scores + jnp.einsum('qhd,kd->hqk', query_rope, key_rope, precision=precision_highest)) * score_scale
    scores = lower_backward(scores)
    positions = jnp.arange(SEQUENCE_LENGTH, dtype=jnp.int32)
    live_keys = (positions[None, :] <= positions[:, None]) & (positions[None, :] < length_now)
    scores = jnp.where(live_keys[None], scores, -1e+30)
    row_max = lax.optimization_barrier(jnp.max(scores, axis=-1, keepdims=True))
    exponent = jnp.exp(scores - row_max)
    chances = low(exponent / lax.optimization_barrier(jnp.sum(exponent, axis=-1, keepdims=True)))
    return low(lower_backward(jnp.einsum('hqk,khd->qhd', chances, values, precision=precision_highest)))

def expert_group(pieces, gate_weights, up_weights, down_weights):
    hidden_rows, flat_slot, gate_values = pieces
    slot_total = EXPERTS * CAP
    spread = jnp.zeros((slot_total + 1, D), jnp.float32).at[flat_slot.reshape(-1)].add(jnp.repeat(hidden_rows, TOPK, axis=0))
    blocks = spread[:slot_total].reshape(EXPERTS, CAP, D)
    gate_part = lower_backward(jnp.einsum('ecd,edf->ecf', blocks, gate_weights, precision=precision_highest))
    up_part = lower_backward(jnp.einsum('ecd,edf->ecf', blocks, up_weights, precision=precision_highest))
    activated = low(jax.nn.silu(gate_part) * up_part)
    expert_out = lower_backward(jnp.einsum('ecf,efd->ecd', activated, down_weights, precision=precision_highest))
    padded = jnp.concatenate([expert_out.reshape(slot_total, D), jnp.zeros((1, D), jnp.float32)], axis=0)
    return jnp.einsum('tk,tkd->td', gate_values, padded[flat_slot], precision=precision_highest)

def forward(tokens, attn_gain, query_weight, latent_key_weight, latent_gain, kvb_weight, output_weight, ffn_gain, router_matrix, shared_gate_weight, shared_up_weight, shared_down_weight, expert_gate, expert_up, expert_down, lengths, routes, slot_ranks):
    positions = jnp.arange(SEQUENCE_LENGTH, dtype=jnp.int32)
    normed_input = low(normalize(tokens, attn_gain))
    query_rows = lower_backward(jnp.einsum('nvu,ue->nve', normed_input, query_weight, precision=precision_highest)).reshape(SEQUENCE_COUNT, SEQUENCE_LENGTH, HEAD_COUNT, PLAIN_WIDTH + ROTARY_WIDTH)
    latent_state = jnp.einsum('wtk,kx->wtx', normed_input, latent_key_weight, precision=precision_highest)
    compressed = lower_backward(latent_state[..., :RANK])
    key_raw = lower_backward(latent_state[..., RANK:])
    compressed_n = low(normalize(compressed, latent_gain))
    key_rope = low(rotate(key_raw, positions, 1.0))
    query_nope = low(query_rows[..., :PLAIN_WIDTH])
    query_rope = low(rotate(query_rows[..., PLAIN_WIDTH:], positions[:, None], 1.0))
    keyval = low(lower_backward(jnp.einsum('slr,rh->slh', compressed_n, kvb_weight, precision=precision_highest))).reshape(SEQUENCE_COUNT, SEQUENCE_LENGTH, HEAD_COUNT, PLAIN_WIDTH + VALUE_WIDTH)
    mixed_values = lax.map(jax.checkpoint(attend_one), (query_nope, query_rope, keyval[..., :PLAIN_WIDTH], key_rope, keyval[..., PLAIN_WIDTH:], lengths))
    attention_output = lower_backward(jnp.einsum('txc,ci->txi', mixed_values.reshape(SEQUENCE_COUNT, SEQUENCE_LENGTH, HEAD_COUNT * VALUE_WIDTH), output_weight, precision=precision_highest))
    hidden = tokens + attention_output
    hidden_normed = low(normalize(hidden, ffn_gain))
    router_logits = lower_backward(jnp.einsum('ntb,bj->ntj', hidden_normed, router_matrix, precision=precision_highest))
    picked = jnp.take_along_axis(router_logits, routes, axis=-1)
    exponent = jnp.exp(picked - lax.optimization_barrier(jnp.max(picked, axis=-1, keepdims=True)))
    gate_values = exponent / lax.optimization_barrier(jnp.sum(exponent, axis=-1, keepdims=True))
    shared_gate_value = lower_backward(jnp.einsum('hxe,eg->hxg', hidden_normed, shared_gate_weight, precision=precision_highest))
    shared_up_value = lower_backward(jnp.einsum('hxe,eg->hxg', hidden_normed, shared_up_weight, precision=precision_highest))
    shared_activation = low(jax.nn.silu(shared_gate_value) * shared_up_value)
    shared_output = jnp.einsum('tkn,na->tka', shared_activation, shared_down_weight, precision=precision_highest)
    flat_slot = jnp.where(slot_ranks < CAP, routes * CAP + slot_ranks, EXPERTS * CAP).astype(jnp.int32)
    group_count = SEQUENCE_COUNT // SEQ_G
    group_rows = SEQ_G * SEQUENCE_LENGTH
    group_fn = jax.checkpoint(partial(expert_group, gate_weights=expert_gate, up_weights=expert_up, down_weights=expert_down))
    routed = lax.map(group_fn, (hidden_normed.reshape(group_count, group_rows, D), flat_slot.reshape(group_count, group_rows, TOPK), gate_values.reshape(group_count, group_rows, TOPK)))
    branch = lower_backward(routed.reshape(SEQUENCE_COUNT, SEQUENCE_LENGTH, D) + shared_output)
    live_mask = (positions[None, :] < lengths[:, None]).astype(jnp.float32)[..., None]
    return live_mask * (hidden + branch)

def reference(tokens, lengths, routes, slot_ranks, attn_gain, query_weight, latent_key_weight, latent_gain, kvb_weight, output_weight, ffn_gain, router_matrix, shared_gate_weight, shared_up_weight, shared_down_weight, expert_gate, expert_up, expert_down, cotangent):
    floats = tuple((weight_now.astype(jnp.float32) for weight_now in (tokens, attn_gain, query_weight, latent_key_weight, latent_gain, kvb_weight, output_weight, ffn_gain, router_matrix, shared_gate_weight, shared_up_weight, shared_down_weight, expert_gate, expert_up, expert_down)))

    def whole_layer(*inputs):
        return forward(*inputs, lengths, routes, slot_ranks)
    output, pullback = jax.vjp(whole_layer, *floats)
    gradients = pullback(cotangent.astype(jnp.float32))
    return (output.astype(jnp.bfloat16), gradients[0].astype(jnp.bfloat16), gradients[1], gradients[2], gradients[3], gradients[4], gradients[5], gradients[6], gradients[7], gradients[8], gradients[9], gradients[10], gradients[11], gradients[12], gradients[13], gradients[14])
```

```python
import functools

import jax
import jax.numpy as jnp
from jax import lax
from jax.experimental import pallas as pl
from jax.experimental.pallas import tpu as pltpu
from jax.sharding import PartitionSpec as P

HEAD_COUNT = 16
PLAIN_WIDTH = 128
ROTARY_WIDTH = 64
VALUE_WIDTH = 128
RANK = 512
TOPK = 6
SCALE = (PLAIN_WIDTH + ROTARY_WIDTH) ** (-0.5)

epsilon = 1e-06
narrow = jnp.bfloat16
wide = jnp.float32
VMEM_LIMIT = 48 * 1024 * 1024


def normalize(values, gain_row):
    return (
        values * lax.rsqrt(jnp.mean(values * values, axis=-1, keepdims=True) + epsilon) * gain_row
    )


def rotate(values, positions, direction):
    half_width = values.shape[-1] // 2
    frequency = 10000.0 ** (-jnp.arange(half_width, dtype=wide) / half_width)
    angles = positions.astype(wide)[..., None] * frequency
    cosines = jnp.cos(angles)
    sines = jnp.sin(angles) * direction
    first_half = values[..., :half_width]
    second_half = values[..., half_width:]
    return jnp.concatenate(
        [first_half * cosines - second_half * sines, first_half * sines + second_half * cosines],
        axis=-1,
    )


def dot(a, b, dims, out=wide):
    return lax.dot_general(a, b, (dims, ((), ())), preferred_element_type=wide).astype(out)


NN = ((1,), (0,))
NT = ((1,), (1,))
TN = ((0,), (0,))


def without(kernel, inputs, waits):
    def body(*refs):
        kernel(*refs[:inputs], *refs[inputs + len(waits) :])

    return body


def waiting(waits):
    return [pl.BlockSpec(memory_space=pl.ANY)] * len(waits)


def swap_halves(values):
    lane = lax.broadcasted_iota(jnp.int32, values.shape, 1)
    count, half = values.shape[1], ROTARY_WIDTH // 2
    return jnp.where(
        lane % ROTARY_WIDTH < half,
        pltpu.roll(values, count - half, 1),
        pltpu.roll(values, half, 1),
    )


def rotary_tables(positions, columns):
    half = ROTARY_WIDTH // 2
    frequency = 10000.0 ** (-jnp.arange(half, dtype=wide) / half)
    angles = positions.astype(wide)[:, None] * frequency
    cosines, sines = jnp.cos(angles), jnp.sin(angles)
    repeats = columns // ROTARY_WIDTH
    return (
        jnp.concatenate([cosines, cosines] * repeats, axis=1),
        jnp.concatenate([-sines, sines] * repeats, axis=1),
    )


def project_kernel(rows, weights, cosines, sines, nope, rope):
    step = pl.program_id(0)
    out = dot(rows[...], weights[...], NN)

    @pl.when(step < HEAD_COUNT * PLAIN_WIDTH // 512)
    def _():
        nope[...] = out.astype(narrow)

    @pl.when(step >= HEAD_COUNT * PLAIN_WIDTH // 512)
    def _():
        turned = out * jnp.concatenate([cosines[...]] * 4, axis=1)
        turned += swap_halves(out) * jnp.concatenate([sines[...]] * 4, axis=1)
        rope[...] = turned.astype(narrow)


def project(rows, weights, cosines, sines):
    count, width = rows.shape
    plain = HEAD_COUNT * PLAIN_WIDTH // 512
    turned = HEAD_COUNT * ROTARY_WIDTH // 512
    return pl.pallas_call(
        project_kernel,
        grid=(plain + turned,),
        in_specs=[
            pl.BlockSpec((count, width), lambda j: (0, 0)),
            pl.BlockSpec((width, 512), lambda j: (0, j)),
            pl.BlockSpec((count, 128), lambda j: (0, 0)),
            pl.BlockSpec((count, 128), lambda j: (0, 0)),
        ],
        out_specs=[
            pl.BlockSpec((count, 512), lambda j: (0, jnp.minimum(j, plain - 1))),
            pl.BlockSpec((count, 512), lambda j: (0, jnp.maximum(j - plain, 0))),
        ],
        out_shape=[
            jax.ShapeDtypeStruct((count, 512 * plain), narrow),
            jax.ShapeDtypeStruct((count, 512 * turned), narrow),
        ],
        compiler_params=pltpu.CompilerParams(vmem_limit_bytes=VMEM_LIMIT),
        cost_estimate=pl.CostEstimate(
            flops=2 * count * width * 512 * (plain + turned),
            bytes_accessed=2 * width * 512 * (plain + turned),
            transcendentals=0,
        ),
    )(rows, weights, cosines, sines)


def pair_half(shape, half):
    lane = lax.broadcasted_iota(jnp.int32, shape, len(shape) - 1)
    return (lane // ROTARY_WIDTH) == half


def attend_kernel(qn, qr, latent, rope, kvb, key_pos, limit, mixed, log_sum, keyval):
    kv = dot(latent[0], kvb_block(kvb), NN, narrow)
    keyval[0] = kv
    live = key_pos[...] <= limit[0]
    rope_keys = rope[0]
    for half in range(2):
        lo = half * 256
        keys = jnp.concatenate([kv[:, lo : lo + 128], rope_keys], axis=1)
        rope_rows = jnp.where(pair_half(qr.shape[1:], half), qr[0], jnp.zeros_like(qr[0]))
        queries = jnp.concatenate([qn[0, :, half * 128 : half * 128 + 128], rope_rows], axis=1)
        scores = jnp.where(live, dot(queries, keys, NT) * SCALE, -1e30)
        row_max = jnp.max(scores, axis=-1, keepdims=True)
        exponent = jnp.exp(scores - row_max)
        row_sum = jnp.sum(exponent, axis=-1, keepdims=True)
        chances = (exponent * (1.0 / row_sum)).astype(narrow)
        rows = dot(chances, kv[:, lo + 128 : lo + 256], NN, narrow)
        mixed[0, :, half * 128 : half * 128 + 128] = rows
        log_sum[0, :, half * 128 : half * 128 + 128] = jnp.broadcast_to(
            row_max + jnp.log(row_sum), rows.shape
        )


def kvb_spec(weights, first, columns):
    count, quarters, rows, _ = weights.shape
    per_piece = quarters * columns // 512
    return pl.BlockSpec(
        (count, 512 // columns, rows, columns),
        lambda p, s: (0, p % per_piece, 0, first // columns + p // per_piece),
    )


def kvb_block(kvb):
    return jnp.concatenate(
        [kvb[:, q].reshape(RANK, kvb.shape[3]) for q in range(kvb.shape[1])], axis=1
    )


def attend(qn, qr, latent, weights, kvb_first, kvb_columns, key_pos, limit):
    seqs, rows, width = qn.shape
    keys = latent.shape[1]
    pairs = HEAD_COUNT // 2
    kv_width = HEAD_COUNT * (PLAIN_WIDTH + VALUE_WIDTH)
    return pl.pallas_call(
        attend_kernel,
        grid=(pairs, seqs),
        in_specs=[
            pl.BlockSpec((1, rows, 256), lambda p, s: (s, 0, p)),
            pl.BlockSpec((1, rows, 128), lambda p, s: (s, 0, p)),
            pl.BlockSpec((1, keys, RANK), lambda p, s: (s, 0, 0)),
            pl.BlockSpec((1, keys, 128), lambda p, s: (s, 0, RANK // 128)),
            kvb_spec(weights, kvb_first, kvb_columns),
            pl.BlockSpec((1, keys), lambda p, s: (0, 0)),
            pl.BlockSpec((1, rows, 1), lambda p, s: (s, 0, 0)),
        ],
        out_specs=[
            pl.BlockSpec((1, rows, 256), lambda p, s: (s, 0, p)),
            pl.BlockSpec((1, rows, 256), lambda p, s: (s, 0, p)),
            pl.BlockSpec((1, keys, 512), lambda p, s: (s, 0, p)),
        ],
        out_shape=[
            jax.ShapeDtypeStruct((seqs, rows, width), narrow),
            jax.ShapeDtypeStruct((seqs, rows, width), wide),
            jax.ShapeDtypeStruct((seqs, keys, kv_width), narrow),
        ],
        compiler_params=pltpu.CompilerParams(vmem_limit_bytes=VMEM_LIMIT),
        cost_estimate=pl.CostEstimate(
            flops=2 * seqs * HEAD_COUNT * keys * (RANK * 256 + rows * 384),
            bytes_accessed=2 * seqs * keys * kv_width,
            transcendentals=seqs * HEAD_COUNT * rows * keys,
        ),
    )(qn, qr, latent, latent, weights, key_pos, limit)


def attend_back_kernel(
    qn, qr, latent, rope, kvb, keyval, grad_mixed, log_sum, key_pos, limit,
    cosines, sines, latents_before, grad_qn, grad_qr, grad_latents, grad_kvb, grad_latent, grad_rope,
):
    pair = pl.program_id(0)
    seq = pl.program_id(1)
    kv = keyval[0]
    live = key_pos[...] <= limit[0]
    rope_keys = rope[0]
    grads = []
    rope_queries = []
    rope_total = None
    for half in range(2):
        lo = half * 256
        values = kv[:, lo + 128 : lo + 256]
        keys = jnp.concatenate([kv[:, lo : lo + 128], rope_keys], axis=1)
        rope_rows = jnp.where(pair_half(qr.shape[1:], half), qr[0], jnp.zeros_like(qr[0]))
        queries = jnp.concatenate([qn[0, :, half * 128 : half * 128 + 128], rope_rows], axis=1)
        sums = log_sum[0, :, half * 128 : half * 128 + 1]
        scores = jnp.where(live, dot(queries, keys, NT) * SCALE, -1e30)
        chances = jnp.exp(scores - sums)
        grad_rows = grad_mixed[0, :, half * 128 : half * 128 + 128]
        grad_chances = dot(grad_rows, values, NT)
        inner = jnp.sum(chances * grad_chances, axis=-1, keepdims=True)
        grad_scores = (chances * (grad_chances - inner)).astype(narrow)
        grad_queries = dot(grad_scores, keys, NN) * SCALE
        grad_qn[0, :, half * 128 : half * 128 + 128] = grad_queries[:, :128].astype(narrow)
        rope_queries.append(grad_queries[:, 128:])
        grad_keys = dot(grad_scores, queries, TN) * SCALE
        grad_values = dot(chances.astype(narrow), grad_rows, TN)
        grads += [grad_keys[:, :128].astype(narrow), grad_values.astype(narrow)]
        rope_part = grad_keys[:, 128:]
        rope_total = rope_part if rope_total is None else rope_total + rope_part
    rope_rows = jnp.where(pair_half(qr.shape[1:], 0), rope_queries[0], rope_queries[1])
    rope_rows = rope_rows * cosines[...] - swap_halves(rope_rows) * sines[...]
    grad_qr[0] = rope_rows.astype(narrow)
    grad_keyval = jnp.concatenate(grads, axis=1)
    latent_part = dot(grad_keyval, kvb_block(kvb), NT)
    kvb_part = dot(latent[0], grad_keyval, TN)

    @pl.when(pair == 0)
    def _():
        grad_latent[seq] = latent_part + latents_before[seq, :, :RANK].astype(wide)
        grad_rope[seq] = rope_total + latents_before[seq, :, RANK:].astype(wide)

    @pl.when(pair > 0)
    def _():
        grad_latent[seq] += latent_part
        grad_rope[seq] += rope_total

    @pl.when(pair == pl.num_programs(0) - 1)
    def _():
        grad_latents[seq, :, :RANK] = grad_latent[seq].astype(narrow)
        rope_sum = grad_rope[seq]
        rope_sum = rope_sum + pltpu.roll(rope_sum, ROTARY_WIDTH, 1)
        grad_latents[seq, :, RANK:] = jnp.where(
            pair_half(rope_sum.shape, 0), rope_sum, 0.0
        ).astype(narrow)

    columns = grad_kvb.shape[3]
    for q in range(grad_kvb.shape[1]):
        part = kvb_part[:, q * columns : (q + 1) * columns].reshape(
            grad_kvb.shape[0], grad_kvb.shape[2], columns
        )

        @pl.when(seq == 0)
        def _(q=q, part=part):
            grad_kvb[:, q] = part

        @pl.when(seq > 0)
        def _(q=q, part=part):
            grad_kvb[:, q] += part


def attend_back(
    qn, qr, latent, weights, kvb_first, kvb_columns, keyval, grad_mixed, log_sum, key_pos, limit,
    cosines, sines, latents_before, first, pairs, waits=(),
):
    seqs, rows, _ = qn.shape
    keys = latent.shape[1]
    width = pairs * 256
    kv = kvb_spec(weights, kvb_first, kvb_columns)
    return pl.pallas_call(
        without(attend_back_kernel, 13, waits),
        grid=(pairs, seqs),
        in_specs=[
            pl.BlockSpec((1, rows, 256), lambda p, s: (s, 0, p + first)),
            pl.BlockSpec((1, rows, 128), lambda p, s: (s, 0, p + first)),
            pl.BlockSpec((1, keys, RANK), lambda p, s: (s, 0, 0)),
            pl.BlockSpec((1, keys, 128), lambda p, s: (s, 0, RANK // 128)),
            pl.BlockSpec(kv.block_shape, lambda p, s: kv.index_map(p + first, s)),
            pl.BlockSpec((1, keys, 512), lambda p, s: (s, 0, p + first)),
            pl.BlockSpec((1, rows, 256), lambda p, s: (s, 0, p + first)),
            pl.BlockSpec((1, rows, 256), lambda p, s: (s, 0, p + first)),
            pl.BlockSpec((1, keys), lambda p, s: (0, 0)),
            pl.BlockSpec((1, rows, 1), lambda p, s: (s, 0, 0)),
            pl.BlockSpec((rows, 128), lambda p, s: (0, 0)),
            pl.BlockSpec((rows, 128), lambda p, s: (0, 0)),
            pl.BlockSpec((seqs, keys, RANK + 128), lambda p, s: (0, 0, 0)),
        ]
        + waiting(waits),
        out_specs=[
            pl.BlockSpec((1, rows, 256), lambda p, s: (s, 0, p)),
            pl.BlockSpec((1, rows, 128), lambda p, s: (s, 0, p)),
            pl.BlockSpec((seqs, keys, RANK + 128), lambda p, s: (0, 0, 0)),
            kvb_spec(weights, 0, kvb_columns),
        ],
        out_shape=[
            jax.ShapeDtypeStruct((seqs, rows, width), narrow),
            jax.ShapeDtypeStruct((seqs, rows, width // 2), narrow),
            jax.ShapeDtypeStruct((seqs, keys, RANK + 128), narrow),
            jax.ShapeDtypeStruct(weights.shape[:3] + (pairs * 512 // weights.shape[1],), wide),
        ],
        scratch_shapes=[
            pltpu.VMEM((seqs, keys, RANK), wide),
            pltpu.VMEM((seqs, keys, 128), wide),
        ],
        compiler_params=pltpu.CompilerParams(vmem_limit_bytes=VMEM_LIMIT),
        cost_estimate=pl.CostEstimate(
            flops=4 * seqs * pairs * keys * (2 * RANK * 256 + rows * 1024),
            bytes_accessed=2 * seqs * keys * pairs * 512,
            transcendentals=2 * seqs * pairs * rows * keys,
        ),
    )(qn, qr, latent, latent, weights, keyval, grad_mixed, log_sum, key_pos, limit, cosines, sines, latents_before, *waits)


def ffn_kernel(pieces, *refs):
    rows_h, rows_g, weight = refs[:pieces], refs[pieces : 2 * pieces], refs[2 * pieces]
    unit_gu, unit_d = refs[2 * pieces + 1], refs[2 * pieces + 2]
    branch, grad_rows = refs[2 * pieces + 3 : 3 * pieces + 3], refs[3 * pieces + 3 : 4 * pieces + 3]
    acts, grad_gate_up, grad_gates, total, grad_total = refs[4 * pieces + 3 :]
    piece = pl.program_id(0)
    step = pl.program_id(1)
    steps = pl.num_programs(1)
    units, hidden, width = unit_d.shape

    def work(source_h, source_g):
        w_gu = unit_gu[...].reshape(2 * units * hidden, width)
        w_d = unit_d[...].reshape(units * hidden, width)
        gate_up = dot(w_gu, source_h[...], NT)
        grad_act = dot(w_d, source_g[...], NT)
        act_parts, grad_parts = [], []
        for k in range(units):
            gate = gate_up[2 * k * hidden : (2 * k + 1) * hidden]
            up = gate_up[(2 * k + 1) * hidden : (2 * k + 2) * hidden]
            part = grad_act[k * hidden : (k + 1) * hidden]
            scale = weight[0, k]
            sigmoid = 1.0 / (1.0 + jnp.exp(-gate))
            silu = gate * sigmoid
            act = silu * up
            grad_gates[0, k] = jnp.sum(act * part, axis=0, keepdims=True)
            act_parts.append((act * scale).astype(narrow))
            part = part * scale
            grad_parts.append((part * up * (sigmoid + silu * (1.0 - sigmoid))).astype(narrow))
            grad_parts.append((part * silu).astype(narrow))
        act_rows = jnp.concatenate(act_parts, axis=0)
        grad_gu = jnp.concatenate(grad_parts, axis=0)
        acts[0] = act_rows.reshape(acts.shape[1:])
        grad_gate_up[0] = grad_gu.reshape(grad_gate_up.shape[1:])
        for first in range(0, width, 1024):
            part = slice(first, first + 1024)
            out = dot(act_rows, w_d[:, part], TN)
            grad = dot(grad_gu, w_gu[:, part], TN)

            @pl.when(step == 0)
            def _(part=part, out=out, grad=grad):
                total[:, part] = out
                grad_total[:, part] = grad

            @pl.when(step > 0)
            def _(part=part, out=out, grad=grad):
                total[:, part] += out
                grad_total[:, part] += grad

    for s in range(pieces):

        @pl.when(piece == s)
        def _(s=s):
            work(rows_h[s], rows_g[s])

            @pl.when(step == steps - 1)
            def _():
                branch[s][...] = total[...].astype(narrow)
                grad_rows[s][...] = grad_total[...].astype(narrow)


def feed_forward(rows_h, rows_g, weights, unit_rows, waits=()):
    pieces = len(rows_h)
    count, width = rows_h[0].shape
    units, hidden, _ = unit_rows.shape
    hidden = hidden // 3
    block = min(units, 4)
    whole = pl.BlockSpec((count, width), lambda s, j: (0, 0), pipeline_mode=pl.Buffered(1))

    def units_of(rows, columns):
        return pl.BlockSpec((1, block, rows, columns), lambda s, j: (s, j, 0, 0))

    outs = pl.pallas_call(
        without(functools.partial(ffn_kernel, pieces), 2 * pieces + 3, waits),
        grid=(pieces, units // block),
        in_specs=[whole] * (2 * pieces)
        + [
            units_of(1, count),
            pl.BlockSpec((block, 2 * hidden, width), lambda s, j: (j, 0, 0)),
            pl.BlockSpec((block, hidden, width), lambda s, j: (j, 2, 0)),
        ]
        + waiting(waits),
        out_specs=[whole] * (2 * pieces)
        + [units_of(hidden, count), units_of(2 * hidden, count), units_of(1, count)],
        out_shape=[jax.ShapeDtypeStruct((count, width), narrow)] * (2 * pieces)
        + [
            jax.ShapeDtypeStruct((pieces, units, hidden, count), narrow),
            jax.ShapeDtypeStruct((pieces, units, 2 * hidden, count), narrow),
            jax.ShapeDtypeStruct((pieces, units, 1, count), wide),
        ],
        scratch_shapes=[pltpu.VMEM((count, width), wide), pltpu.VMEM((count, width), wide)],
        compiler_params=pltpu.CompilerParams(vmem_limit_bytes=60 * 1024 * 1024),
        cost_estimate=pl.CostEstimate(
            flops=12 * pieces * units * hidden * count * width,
            bytes_accessed=pieces * (6 * units * hidden * width + 8 * count * width),
            transcendentals=pieces * units * hidden * count,
        ),
    )(*rows_h, *rows_g, jnp.stack(weights), unit_rows, unit_rows, *waits)
    return [
        (outs[s], outs[pieces + s], outs[2 * pieces], outs[2 * pieces + 1], outs[2 * pieces + 2][s], s)
        for s in range(pieces)
    ]


def weight_grad_kernel(pieces, joined, order, *refs):
    rows_h, rows_g = refs[:pieces], refs[pieces : 2 * pieces]
    acts, grads = refs[2 * pieces : 4 * pieces], refs[4 * pieces : 6 * pieces]
    out = refs[6 * pieces + joined]
    hidden = acts[0].shape[2]
    for k in range(2):
        gate_up = sum(
            dot(grads[2 * s + k][0, 0], rows_h[s][...], NN) for s in range(pieces)
        )
        down = sum(dot(acts[2 * s + k][0, 0], rows_g[s][...], NN) for s in range(pieces))
        if joined:
            before = refs[6 * pieces]
            gate_up += before[k, : 2 * hidden].astype(wide)
            down += before[k, 2 * hidden :].astype(wide)
        out[k, : 2 * hidden] = gate_up.astype(narrow)
        out[k, 2 * hidden :] = down.astype(narrow)


def weight_grads(found, rows_h, rows_g, order, before=None, waits=()):
    pieces, units = len(found), order.shape[0]
    _, _, hidden, count = found[0][2].shape
    width = rows_h[0].shape[1]
    joined = 0 if before is None else 1
    whole = pl.BlockSpec(
        (count, width), lambda j, order: (0, 0), pipeline_mode=pl.Buffered(1)
    )
    pair = pl.BlockSpec((2, 3 * hidden, width), lambda j, order: (j, 0, 0))

    def units_of(rows, at):
        return [
            pl.BlockSpec((1, 1, rows, count), lambda j, order, k=k: (at, order[2 * j + k], 0, 0))
            for k in range(2)
        ]

    return pl.pallas_call(
        without(
            functools.partial(weight_grad_kernel, pieces, joined), 6 * pieces + joined + 1, waits
        ),
        grid_spec=pltpu.PrefetchScalarGridSpec(
            num_scalar_prefetch=1,
            grid=(units // 2,),
            in_specs=[whole] * (2 * pieces)
            + [spec for item in found for spec in units_of(hidden, item[5])]
            + [spec for item in found for spec in units_of(2 * hidden, item[5])]
            + [pair] * joined
            + waiting(waits),
            out_specs=pair,
        ),
        out_shape=jax.ShapeDtypeStruct((units, 3 * hidden, width), narrow),
        compiler_params=pltpu.CompilerParams(vmem_limit_bytes=60 * 1024 * 1024),
        cost_estimate=pl.CostEstimate(
            flops=6 * pieces * units * hidden * count * width,
            bytes_accessed=6 * units * hidden * (width + pieces * count)
            + 4 * pieces * count * width,
            transcendentals=0,
        ),
    )(
        order,
        *rows_h,
        *rows_g,
        *[item[2] for item in found for _ in range(2)],
        *[item[3] for item in found for _ in range(2)],
        *([] if before is None else [before]),
        *waits,
    )


def zero_of(*others):
    firsts = [lax.slice(o, [0] * o.ndim, [1] * o.ndim).reshape(()) for o in others]
    return sum(jnp.where(first != first, 1.0, 0.0) for first in firsts)


def after(values, *others):
    if not others:
        return values
    return (values.astype(wide) + zero_of(*others)).astype(values.dtype)


def hop(values):
    count = lax.axis_size("tp")
    return lax.ppermute(values, "tp", [(i, (i + 1) % count) for i in range(count)])


def ring_gather(values):
    pieces = [values]
    for _ in range(lax.axis_size("tp") - 1):
        pieces.append(hop(pieces[-1]))
    return pieces


def ring_scatter(pieces):
    total = pieces[1].astype(narrow)
    for piece in pieces[2:]:
        total = (hop(total).astype(wide) + piece).astype(narrow)
    return hop(total).astype(wide) + pieces[0]


def cross_scatter(pieces):
    return sum((item.astype(wide) for item in cross_moves(pieces)), pieces[0].astype(wide))


def scatter_tp(values, axis, rows):
    count, rank = lax.axis_size("tp"), lax.axis_index("tp")
    size = values.shape[axis] // count
    placed = jnp.concatenate(
        [
            lax.dynamic_slice_in_dim(
                values, (rank + count - d) % count * size, size, axis
            ).reshape(rows, -1)
            for d in range(count)
        ],
        axis=0,
    )
    return lax.psum_scatter(placed, "tp", scatter_dimension=0, tiled=True).astype(wide)


def cross_moves(pieces):
    count = lax.axis_size("tp")
    return [
        lax.ppermute(pieces[s].astype(narrow), "tp", [(i, (i - s) % count) for i in range(count)])
        for s in range(1, count)
    ]


def cross_sum(values):
    count, rank = lax.axis_size("tp"), lax.axis_index("tp")
    values = values.astype(narrow)
    pieces = [values] + [
        lax.ppermute(values, "tp", [(i, (i + s) % count) for i in range(count)])
        for s in range(1, count)
    ]
    stacked = jnp.stack(pieces)
    return sum(
        lax.dynamic_index_in_dim(stacked, (rank + count - r) % count, 0, False).astype(wide)
        for r in range(count)
    )


def swap(values, mask):
    return lax.ppermute(values, "fsdp", [(i, i ^ mask) for i in range(lax.axis_size("fsdp"))])


def gather_fsdp(values, axis=0):
    return lax.all_gather(values, "fsdp", axis=axis, tiled=True)


def scatter_fsdp(values, axis=0):
    return lax.psum_scatter(values.astype(narrow), "fsdp", scatter_dimension=axis, tiled=True)


def relative_masks(count):
    return [0, 2, 6, 4] if count == 8 else list(range(0, count, 2))


def relative_blocks(values, other, axis):
    count, rank = lax.axis_size("fsdp"), lax.axis_index("fsdp")
    size = values.shape[axis] // count
    return [
        lax.dynamic_slice_in_dim(values, (rank ^ (mask + other)) * size, size, axis)
        for mask in relative_masks(count)
    ]


class Scatter:
    def __init__(self, sent):
        self.sent = sent.astype(narrow)
        self.received = swap(self.sent, 1)

    def join(self, make, *others):
        part = make(self.received, zero_of(*others) if others else None)
        half = part.shape[1] // 2
        self.part = part
        self.from_x, self.from_y = swap(part[1:3, :half], 2), swap(part[2:4, half:], 4)

    def turn(self, *others):
        half = self.part.shape[1] // 2
        zero = zero_of(*others) if others else 0.0
        self.own_top = self.part[0, :half].astype(wide) + self.from_x[0]
        self.own_low = self.part[0, half:].astype(wide) + self.from_y[1]
        top = (self.part[3, :half].astype(wide) + self.from_x[1] + zero).astype(narrow)
        low = (self.part[1, half:].astype(wide) + self.from_y[0] + zero).astype(narrow)
        self.turned = top
        self.last_top, self.last_low = swap(top, 4), swap(low, 2)

    def end(self, *others):
        zero = zero_of(*others) if others else 0.0
        return jnp.concatenate(
            [self.own_top + self.last_top + zero, self.own_low + self.last_low + zero], axis=0
        )


class WholeScatter:
    def __init__(self, values, axis):
        self.sent = self.part = self.turned = values.astype(narrow)
        self.axis = axis

    def join(self, make, *others):
        pass

    def turn(self, *others):
        pass

    def end(self, *others):
        total = scatter_fsdp(self.sent, self.axis).astype(wide)
        return total + zero_of(*others) if others else total


def joiner(make):
    def join(received, zero):
        total = make(0) + received.astype(wide)
        return (total if zero is None else total + zero).astype(narrow)

    return join


def scatter_product(rows, columns, joined=None):
    count = lax.axis_size("fsdp")
    if count != 8:
        out = dot(rows, columns, TN, narrow)
        if joined is not None:
            out = jnp.concatenate([out, joined.astype(narrow)], axis=1)
        return WholeScatter(out, 0), None

    def make(other):
        chosen = jnp.concatenate(relative_blocks(rows, other, 1), axis=1)
        return dot(chosen, columns, TN).reshape(count // 2, -1, columns.shape[1])

    def more(other):
        return jnp.stack(relative_blocks(joined, other, 0))

    if joined is None:
        return Scatter(make(1)), joiner(make)

    def join(received, zero):
        cut = columns.shape[1]
        zero = 0.0 if zero is None else zero
        return jnp.concatenate(
            [
                (make(0) + received[..., :cut].astype(wide) + zero).astype(narrow),
                (more(0) + received[..., cut:].astype(wide)).astype(narrow),
            ],
            axis=2,
        )

    return Scatter(jnp.concatenate([make(1).astype(narrow), more(1).astype(narrow)], axis=2)), join


def scatter_values(values, axis):
    if lax.axis_size("fsdp") != 8:
        return WholeScatter(values, axis), None

    def make(other):
        return jnp.stack(relative_blocks(values, other, axis))

    return Scatter(make(1)), joiner(make)


def on_device(
    tokens,
    lengths,
    routes,
    slot_ranks,
    attn_gain,
    query_weight,
    latent_key_weight,
    latent_gain,
    kvb_weight,
    output_weight,
    ffn_gain,
    router_matrix,
    shared_gate_weight,
    shared_up_weight,
    shared_down_weight,
    expert_gate,
    expert_up,
    expert_down,
    cotangent,
):
    tp_count = lax.axis_size("tp")
    tp_rank = lax.axis_index("tp")
    fsdp_count = lax.axis_size("fsdp")
    seq_count, local_len, width = tokens.shape
    seq_len = local_len * tp_count
    group_rows = seq_count * seq_len
    own_rows = seq_count * local_len
    own_experts = expert_gate.shape[0]
    expert_count = own_experts * fsdp_count
    capacity = 4 * group_rows // expert_count
    ffe = expert_gate.shape[2]
    sff = shared_gate_weight.shape[1]
    head_local = HEAD_COUNT // tp_count
    own_first = tp_rank * local_len
    own_positions = own_first + jnp.arange(local_len, dtype=jnp.int32)
    rel_rank = [(tp_rank + tp_count - s) % tp_count for s in range(tp_count)]
    key_pos = jnp.concatenate(
        [r * local_len + jnp.arange(local_len, dtype=jnp.int32) for r in rel_rank]
    )
    limit = jnp.minimum(own_positions[None, :], lengths[:, None] - 1)[..., None]

    shard = attn_gain.shape[0]
    latent_shard = latent_gain.shape[0]
    latent_width = latent_key_weight.shape[1]
    gain_rows = [latent_width, latent_width + 8, latent_width + 16]
    router_first = latent_width + 24
    small_rows = -(-(router_first + expert_count) // 32) * 32

    def small_stack(latent_key, attn, ffn, latent, router):
        rows = [latent_key]
        for gain in (attn, ffn, latent):
            rows.append(jnp.pad(gain[None], ((0, 7), (0, 0))))
        rows += [router]
        if small_rows > router_first + expert_count:
            rows.append(
                jnp.zeros((small_rows - router_first - expert_count, router.shape[1]), router.dtype)
            )
        return jnp.concatenate(rows, axis=0)

    small_shard = small_stack(
        latent_key_weight.T,
        attn_gain,
        ffn_gain,
        jnp.pad(latent_gain, (0, shard - latent_shard)),
        router_matrix.T,
    )
    small_all = gather_fsdp(small_shard, axis=1)
    latent_key_whole = small_all[:latent_width]
    attn_scale = small_all[gain_rows[0]].astype(wide)
    ffn_scale = small_all[gain_rows[1]].astype(wide)
    latent_scale = (
        small_all[gain_rows[2]]
        .reshape(fsdp_count, shard)[:, :latent_shard]
        .reshape(-1)
        .astype(wide)
    )
    router_t = small_all[router_first : router_first + expert_count]

    query_heads = query_weight.reshape(shard, head_local, PLAIN_WIDTH + ROTARY_WIDTH)
    nope_cols, rope_cols = head_local * PLAIN_WIDTH, head_local * ROTARY_WIDTH
    query_cols, output_cols = query_weight.shape[1], output_weight.shape[0]
    kv_rows, kv_cols = kvb_weight.shape
    quarters = shard // kv_rows
    kvb_columns = kv_cols // quarters
    attention_shard = jnp.concatenate(
        [
            query_heads[..., :PLAIN_WIDTH].reshape(shard, -1),
            query_heads[..., PLAIN_WIDTH:].reshape(shard, -1),
            output_weight.T,
            jnp.concatenate(jnp.split(kvb_weight, quarters, axis=1), axis=0),
        ],
        axis=1,
    )
    attention_pieces = ring_gather(after(attention_shard, small_shard))
    cuts = [0, nope_cols, query_cols, query_cols + output_cols, query_cols + output_cols + kvb_columns]
    attention_joined = jnp.concatenate(
        [
            piece[:, first:last]
            for first, last in zip(cuts[:-1], cuts[1:])
            for piece in attention_pieces
        ],
        axis=1,
    )
    attention_all = gather_fsdp(attention_joined)
    query_end = tp_count * query_cols
    kvb_first = query_end + tp_count * output_cols
    query_whole = attention_all[:, :query_end]
    output_whole = attention_all[:, query_end:kvb_first]
    kvb_whole = attention_all.reshape(fsdp_count, quarters, kv_rows, -1)

    token_rows = tokens.reshape(own_rows, width).astype(wide)
    normed = normalize(token_rows, attn_scale).astype(narrow)
    latent_rows = dot(normed, latent_key_whole, NT)
    compressed = latent_rows[:, :RANK]
    compressed_n = normalize(compressed, latent_scale).astype(narrow)
    row_positions = jnp.concatenate([own_positions] * seq_count)
    key_rope_own = rotate(latent_rows[:, RANK:], row_positions, 1.0).astype(narrow)
    latent_pieces = ring_gather(
        after(
            jnp.concatenate([compressed_n, key_rope_own, key_rope_own], axis=1),
            attention_joined,
        )
    )
    latent_all = jnp.concatenate(
        [piece.reshape(seq_count, local_len, -1) for piece in latent_pieces], axis=1
    )

    split = 2 if ffe % 32 == 0 else 1
    unit = ffe // split
    shared_units = sff // unit
    shared_shard = jnp.concatenate(
        [
            shared_gate_weight.T.reshape(shared_units, unit, shard),
            shared_up_weight.T.reshape(shared_units, unit, shard),
            shared_down_weight.reshape(shared_units, unit, shard),
        ],
        axis=1,
    )
    weights = [
        gather_fsdp(after(shared_shard.reshape(3 * sff, shard), latent_pieces[2]), axis=1).reshape(
            shared_units, 3 * unit, width
        )
    ]
    gate_rows, up_rows = expert_gate[0].T, expert_up[0].T
    for g in range(split):
        part = slice(g * unit, (g + 1) * unit)
        shard_rows = jnp.concatenate([gate_rows[part], up_rows[part], expert_down[0, part]], axis=0)
        weights.append(
            gather_fsdp(after(shard_rows, latent_pieces[1 + 2 * g])).reshape(
                expert_count, 3 * unit, width
            )
        )

    live_mask = (own_positions[None, :] < lengths[:, None]).astype(wide).reshape(own_rows, 1)
    grad_out = live_mask * cotangent.reshape(own_rows, width).astype(wide)
    grad_pieces = ring_gather(after(grad_out.astype(narrow), latent_all))

    cosines, sines = rotary_tables(own_positions, 128)
    query_nope, query_rope = project(
        normed,
        attention_all,
        jnp.concatenate([cosines] * seq_count),
        jnp.concatenate([sines] * seq_count),
    )
    query_nope = query_nope.reshape(seq_count, local_len, -1)
    query_rope = query_rope.reshape(seq_count, local_len, -1)
    key_row = key_pos[None, :]
    mixed, log_sums, keyval = attend(
        query_nope, query_rope, latent_all, kvb_whole, kvb_first, kvb_columns,
        key_row, limit
    )
    mixed = mixed.reshape(own_rows, -1)
    hidden = token_rows + dot(mixed, output_whole, NT)
    hidden_normed = normalize(hidden, ffn_scale).astype(narrow)
    hidden_pieces = ring_gather(hidden_normed)

    expert_ids = jnp.arange(expert_count, dtype=jnp.int32)[:, None, None]
    ones = jnp.ones((shared_units, 1, own_rows), wide)
    gate_tables = []
    for s in range(tp_count):
        first = rel_rank[s] * local_len
        route_t = lax.dynamic_slice_in_dim(routes, first, local_len, 1).reshape(own_rows, TOPK).T
        rank_t = lax.dynamic_slice_in_dim(slot_ranks, first, local_len, 1).reshape(own_rows, TOPK).T
        hits = route_t[None] == expert_ids
        chosen = jnp.any(hits, axis=1)
        kept = jnp.any(hits & (rank_t < capacity)[None], axis=1).astype(wide)
        logits = dot(router_t, hidden_pieces[s], NT)
        picked = jnp.where(chosen, logits, -1e30)
        exponent = jnp.where(chosen, jnp.exp(picked - jnp.max(picked, axis=0, keepdims=True)), 0.0)
        gates = exponent / jnp.sum(exponent, axis=0, keepdims=True)
        gate_tables.append((gates, kept))

    chunks = range(tp_count)
    results = {}
    previous = []

    def run(group, which, *waits):
        tables = [
            ones if group == 0 else (gate_tables[s][0] * gate_tables[s][1])[:, None, :]
            for s in which
        ]
        found = feed_forward(
            [hidden_pieces[s] for s in which],
            [grad_pieces[s] for s in which],
            tables,
            weights[group],
            [*previous, *waits],
        )
        for s, item in zip(which, found):
            results[group, s] = item
        previous[:] = [found[0][4]]

    def grads_of(group, units, *others, before=None):
        out = weight_grads(
            [results[group, s] for s in chunks],
            hidden_pieces,
            grad_pieces,
            units,
            before,
            [*previous, *others],
        )
        previous[:] = [out]
        return out

    def finish_piece(s, *others):
        found = [results[g, s] for g in range(split + 1)]
        branch = sum(item[0].astype(wide) for item in found).astype(narrow)
        gates, kept = gate_tables[s]
        grad_gates = sum(item[4][:, 0] for item in found[1:]) * kept
        logits = (
            gates * (grad_gates - jnp.sum(gates * grad_gates, axis=0, keepdims=True))
        ).astype(narrow)
        grad_hidden = sum(item[1].astype(wide) for item in found)
        if others:
            grad_hidden += zero_of(*others)
        return branch, grad_hidden + dot(logits, router_t, TN), logits

    last_order = list(chunks[1:]) + [0]
    pairs = [chunks[s : s + 2] for s in range(0, tp_count, 2)]
    if split == 2:
        run(1, [0])
        run(1, [1])
    run(0, [0])
    run(0, [1], hidden_pieces[2])
    for which in pairs[1:]:
        if split == 2:
            for s in which:
                run(1, [s])
        run(0, which)
    all_units = jnp.arange(expert_count, dtype=jnp.int32)
    shared_sum = scatter_fsdp(
        grads_of(0, jnp.arange(shared_units, dtype=jnp.int32)).reshape(3 * sff, width), 1
    )
    first_sum = None
    if split == 2:
        first_sum = scatter_fsdp(grads_of(1, all_units).reshape(-1, width))

    pieces, total = {}, None
    for k, s in enumerate(last_order):
        if k == 2:
            previous.append(shared_sum)
        if k == tp_count - 1:
            pieces[last_order[1]] = finish_piece(last_order[1], *previous)
            total = (hop(total).astype(wide) + pieces[last_order[1]][1]).astype(narrow)
            previous.append(total)
        run(split, [s])
        if k == 0:
            pieces[s] = finish_piece(s)
            total = pieces[s][1].astype(narrow)
            previous.append(total)
    for s in last_order[2:-1]:
        pieces[s] = finish_piece(s, *previous)
        total = (hop(total).astype(wide) + pieces[s][1]).astype(narrow)
    previous.append(total)
    if first_sum is not None:
        previous.append(first_sum)
    last_sum = scatter_fsdp(grads_of(split, all_units).reshape(-1, width))
    pieces[0] = finish_piece(0, *previous)
    grad_hidden_own = hop(total).astype(wide) + pieces[0][1]

    hidden_back = jax.vjp(normalize, hidden, ffn_scale)[1]
    grad_hnorm, grad_ffn_gain = hidden_back(grad_hidden_own)
    grad_hidden = grad_out + grad_hnorm
    grad_attn = grad_hidden.astype(narrow)
    branch_total = after(pieces[last_order[0]][0], grad_attn)
    out_scatter, make_out = scatter_product(grad_attn, mixed)
    grad_mixed = dot(after(grad_attn, out_scatter.sent), output_whole, NN, narrow)
    out_scatter.join(make_out, grad_mixed)

    def back(first, pairs, rows, latents_before, waits):
        return attend_back(
            query_nope, query_rope, latent_all, kvb_whole, kvb_first, kvb_columns, keyval,
            rows.reshape(seq_count, local_len, -1), log_sums, key_row, limit,
            cosines, sines, latents_before, first, pairs, waits,
        )

    pairs_half = HEAD_COUNT // 4
    first_qn, first_qr, first_latents, first_kvb = back(
        0, pairs_half, grad_mixed, jnp.zeros_like(latent_all), [out_scatter.part]
    )
    first_query = jnp.concatenate([first_qn, first_qr], axis=-1).reshape(own_rows, -1)
    first_scatter, make_first_query = scatter_product(
        normed, first_query, first_kvb.reshape(width, -1)
    )
    out_scatter.turn(first_scatter.sent)
    branch_total = (
        hop(branch_total).astype(wide) + after(pieces[2][0], out_scatter.turned)
    ).astype(narrow)
    second_qn, second_qr, grad_latent_all, second_kvb = back(
        pairs_half, pairs_half, grad_mixed, first_latents,
        [branch_total, out_scatter.turned, last_sum],
    )

    grad_latent_sum = scatter_tp(grad_latent_all, 1, own_rows)
    second_query = jnp.concatenate([second_qn, second_qr], axis=-1).reshape(own_rows, -1)
    second_scatter, make_second_query = scatter_product(
        normed, second_query, second_kvb.reshape(width, -1)
    )
    out_sum = out_scatter.end(second_scatter.sent)
    first_scatter.join(make_first_query, out_sum)
    second_scatter.join(make_second_query, first_scatter.part)
    half_plain, half_turned = first_qn.shape[2], first_qr.shape[2]
    query_gradient = jnp.concatenate(
        [
            first_query[:, :half_plain],
            second_query[:, :half_plain],
            first_query[:, half_plain:],
            second_query[:, half_plain:],
        ],
        axis=1,
    )
    grad_normed = dot(after(query_gradient, second_scatter.part), query_whole, NT)
    first_scatter.turn(grad_normed)

    latent_back = jax.vjp(normalize, compressed, latent_scale)[1]
    grad_compressed, grad_latent_gain = latent_back(grad_latent_sum[:, :RANK])
    latent_gradient = jnp.concatenate(
        [
            grad_compressed,
            rotate(grad_latent_sum[:, RANK : RANK + ROTARY_WIDTH], row_positions, -1.0),
        ],
        axis=-1,
    ).astype(narrow)
    latent_key_gradient = dot(latent_gradient, normed, TN)
    grad_normed = grad_normed + dot(latent_gradient, latent_key_whole, NN)
    token_back = jax.vjp(normalize, token_rows, attn_scale)[1]
    grad_tnorm, grad_attn_gain = token_back(grad_normed)
    grad_tokens = (grad_hidden + grad_tnorm).astype(narrow).reshape(tokens.shape)

    router_gradient = sum(dot(pieces[s][2], hidden_pieces[s], NN) for s in chunks)

    small_grads = small_stack(
        latent_key_gradient,
        grad_attn_gain,
        grad_ffn_gain,
        jnp.pad(
            grad_latent_gain.reshape(fsdp_count, latent_shard),
            ((0, 0), (0, shard - latent_shard)),
        ).reshape(-1),
        router_gradient,
    )
    small_sum = cross_sum(scatter_fsdp(small_grads, 1))
    second_scatter.turn(small_grads)
    for s in chunks[3:]:
        branch_total = (
            hop(branch_total).astype(wide) + after(pieces[s][0], second_scatter.turned)
        ).astype(narrow)

    first_own = first_scatter.end()
    second_own = second_scatter.end()
    half_query = half_plain + half_turned

    def query_piece(s):
        half = tp_count // 2
        values, at = (first_own, s) if s < half else (second_own, s - half)
        return jnp.concatenate(
            [
                values[:, at * nope_cols : (at + 1) * nope_cols],
                values[:, half_plain + at * rope_cols : half_plain + (at + 1) * rope_cols],
                values[:, half_query + at * kvb_columns : half_query + (at + 1) * kvb_columns],
            ],
            axis=1,
        )

    out_own = cross_scatter(jnp.split(out_sum, tp_count, axis=1)).T
    query_own = cross_scatter([query_piece(s) for s in chunks])
    branch_own = hop(branch_total).astype(wide) + pieces[0][0]
    output = (live_mask * (hidden + branch_own)).astype(narrow).reshape(tokens.shape)
    kvb_own = jnp.concatenate(jnp.split(query_own[:, query_cols:], quarters, axis=0), axis=1)
    query_own = jnp.concatenate(
        [
            query_own[:, :nope_cols].reshape(shard, head_local, PLAIN_WIDTH),
            query_own[:, nope_cols:query_cols].reshape(shard, head_local, ROTARY_WIDTH),
        ],
        axis=-1,
    ).reshape(shard, -1)
    shared_sum = shared_sum.astype(wide).reshape(shared_units, 3, unit, shard)
    expert_sum = [last_sum] if first_sum is None else [first_sum, last_sum]
    expert_sum = jnp.concatenate(
        [item.astype(wide).reshape(3, unit, width) for item in expert_sum], axis=1
    )
    return (
        output,
        grad_tokens,
        small_sum[gain_rows[0]],
        query_own,
        small_sum[:latent_width].T,
        small_sum[gain_rows[2], :latent_shard],
        kvb_own,
        out_own,
        small_sum[gain_rows[1]],
        small_sum[router_first : router_first + expert_count].T,
        shared_sum[:, 0].reshape(sff, shard).T,
        shared_sum[:, 1].reshape(sff, shard).T,
        shared_sum[:, 2].reshape(sff, shard),
        expert_sum[0].T[None],
        expert_sum[1].T[None],
        expert_sum[2][None],
    )


def solution(mesh):
    in_specs = (
        P("fsdp", "tp", None),
        P("fsdp"),
        P("fsdp", None, None),
        P("fsdp", None, None),
        P("fsdp"),
        P("fsdp", "tp"),
        P("fsdp", None),
        P("fsdp"),
        P("fsdp", "tp"),
        P("tp", "fsdp"),
        P("fsdp"),
        P("fsdp", None),
        P("fsdp", "tp"),
        P("fsdp", "tp"),
        P("tp", "fsdp"),
        P("fsdp", None, "tp"),
        P("fsdp", None, "tp"),
        P("fsdp", "tp", None),
        P("fsdp", "tp", None),
    )
    out_specs = (
        P("fsdp", "tp", None),
        P("fsdp", "tp", None),
        P("fsdp"),
        P("fsdp", "tp"),
        P("fsdp", None),
        P("fsdp"),
        P("fsdp", "tp"),
        P("tp", "fsdp"),
        P("fsdp"),
        P("fsdp", None),
        P("fsdp", "tp"),
        P("fsdp", "tp"),
        P("tp", "fsdp"),
        P("fsdp", None, "tp"),
        P("fsdp", None, "tp"),
        P("fsdp", "tp", None),
    )
    return jax.shard_map(
        on_device, mesh=mesh, in_specs=in_specs, out_specs=out_specs, check_vma=False
    )
```

```python
import functools

import jax
import jax.numpy as jnp
from jax import lax
from jax.experimental import pallas as pl
from jax.experimental.pallas import tpu as pltpu
from jax.sharding import PartitionSpec as P

HEAD_COUNT = 16
PLAIN_WIDTH = 128
ROTARY_WIDTH = 64
VALUE_WIDTH = 128
RANK = 512
TOPK = 6
SCALE = (PLAIN_WIDTH + ROTARY_WIDTH) ** (-0.5)

epsilon = 1e-06
narrow = jnp.bfloat16
wide = jnp.float32
VMEM_LIMIT = 48 * 1024 * 1024


def normalize(values, gain_row):
    return (
        values * lax.rsqrt(jnp.mean(values * values, axis=-1, keepdims=True) + epsilon) * gain_row
    )


def rotate(values, positions, direction):
    half_width = values.shape[-1] // 2
    frequency = 10000.0 ** (-jnp.arange(half_width, dtype=wide) / half_width)
    angles = positions.astype(wide)[..., None] * frequency
    cosines = jnp.cos(angles)
    sines = jnp.sin(angles) * direction
    first_half = values[..., :half_width]
    second_half = values[..., half_width:]
    return jnp.concatenate(
        [first_half * cosines - second_half * sines, first_half * sines + second_half * cosines],
        axis=-1,
    )


def dot(a, b, dims, out=wide):
    return lax.dot_general(a, b, (dims, ((), ())), preferred_element_type=wide).astype(out)


NN = ((1,), (0,))
NT = ((1,), (1,))
TN = ((0,), (0,))


def without(kernel, inputs, waits):
    def body(*refs):
        kernel(*refs[:inputs], *refs[inputs + len(waits) :])

    return body


def waiting(waits):
    return [pl.BlockSpec(memory_space=pl.ANY)] * len(waits)


def swap_halves(values):
    lane = lax.broadcasted_iota(jnp.int32, values.shape, 1)
    count, half = values.shape[1], ROTARY_WIDTH // 2
    return jnp.where(
        lane % ROTARY_WIDTH < half,
        pltpu.roll(values, count - half, 1),
        pltpu.roll(values, half, 1),
    )


def rotary_tables(positions, columns):
    half = ROTARY_WIDTH // 2
    frequency = 10000.0 ** (-jnp.arange(half, dtype=wide) / half)
    angles = positions.astype(wide)[:, None] * frequency
    cosines, sines = jnp.cos(angles), jnp.sin(angles)
    repeats = columns // ROTARY_WIDTH
    return (
        jnp.concatenate([cosines, cosines] * repeats, axis=1),
        jnp.concatenate([-sines, sines] * repeats, axis=1),
    )


def project_kernel(rows, weights, cosines, sines, nope, rope):
    step = pl.program_id(0)
    out = dot(rows[...], weights[...], NN)

    @pl.when(step < HEAD_COUNT * PLAIN_WIDTH // 512)
    def _():
        nope[...] = out.astype(narrow)

    @pl.when(step >= HEAD_COUNT * PLAIN_WIDTH // 512)
    def _():
        turned = out * jnp.concatenate([cosines[...]] * 4, axis=1)
        turned += swap_halves(out) * jnp.concatenate([sines[...]] * 4, axis=1)
        rope[...] = turned.astype(narrow)


def project(rows, weights, cosines, sines):
    count, width = rows.shape
    plain = HEAD_COUNT * PLAIN_WIDTH // 512
    turned = HEAD_COUNT * ROTARY_WIDTH // 512
    return pl.pallas_call(
        project_kernel,
        grid=(plain + turned,),
        in_specs=[
            pl.BlockSpec((count, width), lambda j: (0, 0)),
            pl.BlockSpec((width, 512), lambda j: (0, j)),
            pl.BlockSpec((count, 128), lambda j: (0, 0)),
            pl.BlockSpec((count, 128), lambda j: (0, 0)),
        ],
        out_specs=[
            pl.BlockSpec((count, 512), lambda j: (0, jnp.minimum(j, plain - 1))),
            pl.BlockSpec((count, 512), lambda j: (0, jnp.maximum(j - plain, 0))),
        ],
        out_shape=[
            jax.ShapeDtypeStruct((count, 512 * plain), narrow),
            jax.ShapeDtypeStruct((count, 512 * turned), narrow),
        ],
        compiler_params=pltpu.CompilerParams(vmem_limit_bytes=VMEM_LIMIT),
        cost_estimate=pl.CostEstimate(
            flops=2 * count * width * 512 * (plain + turned),
            bytes_accessed=2 * width * 512 * (plain + turned),
            transcendentals=0,
        ),
    )(rows, weights, cosines, sines)


def pair_half(shape, half):
    lane = lax.broadcasted_iota(jnp.int32, shape, len(shape) - 1)
    return (lane // ROTARY_WIDTH) == half


def attend_kernel(qn, qr, latent, rope, kvb, key_pos, limit, mixed, log_sum, keyval):
    kv = dot(latent[0], kvb_block(kvb), NN, narrow)
    keyval[0] = kv
    live = key_pos[...] <= limit[0]
    rope_keys = rope[0]
    for half in range(2):
        lo = half * 256
        keys = jnp.concatenate([kv[:, lo : lo + 128], rope_keys], axis=1)
        rope_rows = jnp.where(pair_half(qr.shape[1:], half), qr[0], jnp.zeros_like(qr[0]))
        queries = jnp.concatenate([qn[0, :, half * 128 : half * 128 + 128], rope_rows], axis=1)
        scores = jnp.where(live, dot(queries, keys, NT) * SCALE, -1e30)
        row_max = jnp.max(scores, axis=-1, keepdims=True)
        exponent = jnp.exp(scores - row_max)
        row_sum = jnp.sum(exponent, axis=-1, keepdims=True)
        chances = (exponent * (1.0 / row_sum)).astype(narrow)
        rows = dot(chances, kv[:, lo + 128 : lo + 256], NN, narrow)
        mixed[0, :, half * 128 : half * 128 + 128] = rows
        log_sum[0, :, half * 128 : half * 128 + 128] = jnp.broadcast_to(
            row_max + jnp.log(row_sum), rows.shape
        )


def kvb_spec(weights, first, columns):
    count, quarters, rows, _ = weights.shape
    per_piece = quarters * columns // 512
    return pl.BlockSpec(
        (count, 512 // columns, rows, columns),
        lambda p, s: (0, p % per_piece, 0, first // columns + p // per_piece),
    )


def kvb_block(kvb):
    return jnp.concatenate(
        [kvb[:, q].reshape(RANK, kvb.shape[3]) for q in range(kvb.shape[1])], axis=1
    )


def attend(qn, qr, latent, weights, kvb_first, kvb_columns, key_pos, limit):
    seqs, rows, width = qn.shape
    keys = latent.shape[1]
    pairs = HEAD_COUNT // 2
    kv_width = HEAD_COUNT * (PLAIN_WIDTH + VALUE_WIDTH)
    return pl.pallas_call(
        attend_kernel,
        grid=(pairs, seqs),
        in_specs=[
            pl.BlockSpec((1, rows, 256), lambda p, s: (s, 0, p)),
            pl.BlockSpec((1, rows, 128), lambda p, s: (s, 0, p)),
            pl.BlockSpec((1, keys, RANK), lambda p, s: (s, 0, 0)),
            pl.BlockSpec((1, keys, 128), lambda p, s: (s, 0, RANK // 128)),
            kvb_spec(weights, kvb_first, kvb_columns),
            pl.BlockSpec((1, keys), lambda p, s: (0, 0)),
            pl.BlockSpec((1, rows, 1), lambda p, s: (s, 0, 0)),
        ],
        out_specs=[
            pl.BlockSpec((1, rows, 256), lambda p, s: (s, 0, p)),
            pl.BlockSpec((1, rows, 256), lambda p, s: (s, 0, p)),
            pl.BlockSpec((1, keys, 512), lambda p, s: (s, 0, p)),
        ],
        out_shape=[
            jax.ShapeDtypeStruct((seqs, rows, width), narrow),
            jax.ShapeDtypeStruct((seqs, rows, width), wide),
            jax.ShapeDtypeStruct((seqs, keys, kv_width), narrow),
        ],
        compiler_params=pltpu.CompilerParams(vmem_limit_bytes=VMEM_LIMIT),
        cost_estimate=pl.CostEstimate(
            flops=2 * seqs * HEAD_COUNT * keys * (RANK * 256 + rows * 384),
            bytes_accessed=2 * seqs * keys * kv_width,
            transcendentals=seqs * HEAD_COUNT * rows * keys,
        ),
    )(qn, qr, latent, latent, weights, key_pos, limit)


def attend_back_kernel(
    qn, qr, latent, rope, kvb, keyval, grad_mixed, log_sum, key_pos, limit,
    cosines, sines, latents_before, grad_qn, grad_qr, grad_latents, grad_kvb, grad_latent, grad_rope,
):
    pair = pl.program_id(0)
    seq = pl.program_id(1)
    kv = keyval[0]
    live = key_pos[...] <= limit[0]
    rope_keys = rope[0]
    grads = []
    rope_queries = []
    rope_total = None
    for half in range(2):
        lo = half * 256
        values = kv[:, lo + 128 : lo + 256]
        keys = jnp.concatenate([kv[:, lo : lo + 128], rope_keys], axis=1)
        rope_rows = jnp.where(pair_half(qr.shape[1:], half), qr[0], jnp.zeros_like(qr[0]))
        queries = jnp.concatenate([qn[0, :, half * 128 : half * 128 + 128], rope_rows], axis=1)
        sums = log_sum[0, :, half * 128 : half * 128 + 1]
        scores = jnp.where(live, dot(queries, keys, NT) * SCALE, -1e30)
        chances = jnp.exp(scores - sums)
        grad_rows = grad_mixed[0, :, half * 128 : half * 128 + 128]
        grad_chances = dot(grad_rows, values, NT)
        inner = jnp.sum(chances * grad_chances, axis=-1, keepdims=True)
        grad_scores = (chances * (grad_chances - inner)).astype(narrow)
        grad_queries = dot(grad_scores, keys, NN) * SCALE
        grad_qn[0, :, half * 128 : half * 128 + 128] = grad_queries[:, :128].astype(narrow)
        rope_queries.append(grad_queries[:, 128:])
        grad_keys = dot(grad_scores, queries, TN) * SCALE
        grad_values = dot(chances.astype(narrow), grad_rows, TN)
        grads += [grad_keys[:, :128].astype(narrow), grad_values.astype(narrow)]
        rope_part = grad_keys[:, 128:]
        rope_total = rope_part if rope_total is None else rope_total + rope_part
    rope_rows = jnp.where(pair_half(qr.shape[1:], 0), rope_queries[0], rope_queries[1])
    rope_rows = rope_rows * cosines[...] - swap_halves(rope_rows) * sines[...]
    grad_qr[0] = rope_rows.astype(narrow)
    grad_keyval = jnp.concatenate(grads, axis=1)
    latent_part = dot(grad_keyval, kvb_block(kvb), NT)
    kvb_part = dot(latent[0], grad_keyval, TN)

    @pl.when(pair == 0)
    def _():
        grad_latent[seq] = latent_part + latents_before[seq, :, :RANK].astype(wide)
        grad_rope[seq] = rope_total + latents_before[seq, :, RANK:].astype(wide)

    @pl.when(pair > 0)
    def _():
        grad_latent[seq] += latent_part
        grad_rope[seq] += rope_total

    @pl.when(pair == pl.num_programs(0) - 1)
    def _():
        grad_latents[seq, :, :RANK] = grad_latent[seq].astype(narrow)
        rope_sum = grad_rope[seq]
        rope_sum = rope_sum + pltpu.roll(rope_sum, ROTARY_WIDTH, 1)
        grad_latents[seq, :, RANK:] = jnp.where(
            pair_half(rope_sum.shape, 0), rope_sum, 0.0
        ).astype(narrow)

    columns = grad_kvb.shape[3]
    for q in range(grad_kvb.shape[1]):
        part = kvb_part[:, q * columns : (q + 1) * columns].reshape(
            grad_kvb.shape[0], grad_kvb.shape[2], columns
        )

        @pl.when(seq == 0)
        def _(q=q, part=part):
            grad_kvb[:, q] = part

        @pl.when(seq > 0)
        def _(q=q, part=part):
            grad_kvb[:, q] += part


def attend_back(
    qn, qr, latent, weights, kvb_first, kvb_columns, keyval, grad_mixed, log_sum, key_pos, limit,
    cosines, sines, latents_before, first, pairs, waits=(),
):
    seqs, rows, _ = qn.shape
    keys = latent.shape[1]
    width = pairs * 256
    kv = kvb_spec(weights, kvb_first, kvb_columns)
    return pl.pallas_call(
        without(attend_back_kernel, 13, waits),
        grid=(pairs, seqs),
        in_specs=[
            pl.BlockSpec((1, rows, 256), lambda p, s: (s, 0, p + first)),
            pl.BlockSpec((1, rows, 128), lambda p, s: (s, 0, p + first)),
            pl.BlockSpec((1, keys, RANK), lambda p, s: (s, 0, 0)),
            pl.BlockSpec((1, keys, 128), lambda p, s: (s, 0, RANK // 128)),
            pl.BlockSpec(kv.block_shape, lambda p, s: kv.index_map(p + first, s)),
            pl.BlockSpec((1, keys, 512), lambda p, s: (s, 0, p + first)),
            pl.BlockSpec((1, rows, 256), lambda p, s: (s, 0, p + first)),
            pl.BlockSpec((1, rows, 256), lambda p, s: (s, 0, p + first)),
            pl.BlockSpec((1, keys), lambda p, s: (0, 0)),
            pl.BlockSpec((1, rows, 1), lambda p, s: (s, 0, 0)),
            pl.BlockSpec((rows, 128), lambda p, s: (0, 0)),
            pl.BlockSpec((rows, 128), lambda p, s: (0, 0)),
            pl.BlockSpec((seqs, keys, RANK + 128), lambda p, s: (0, 0, 0)),
        ]
        + waiting(waits),
        out_specs=[
            pl.BlockSpec((1, rows, 256), lambda p, s: (s, 0, p)),
            pl.BlockSpec((1, rows, 128), lambda p, s: (s, 0, p)),
            pl.BlockSpec((seqs, keys, RANK + 128), lambda p, s: (0, 0, 0)),
            kvb_spec(weights, 0, kvb_columns),
        ],
        out_shape=[
            jax.ShapeDtypeStruct((seqs, rows, width), narrow),
            jax.ShapeDtypeStruct((seqs, rows, width // 2), narrow),
            jax.ShapeDtypeStruct((seqs, keys, RANK + 128), narrow),
            jax.ShapeDtypeStruct(weights.shape[:3] + (pairs * 512 // weights.shape[1],), wide),
        ],
        scratch_shapes=[
            pltpu.VMEM((seqs, keys, RANK), wide),
            pltpu.VMEM((seqs, keys, 128), wide),
        ],
        compiler_params=pltpu.CompilerParams(vmem_limit_bytes=VMEM_LIMIT),
        cost_estimate=pl.CostEstimate(
            flops=4 * seqs * pairs * keys * (2 * RANK * 256 + rows * 1024),
            bytes_accessed=2 * seqs * keys * pairs * 512,
            transcendentals=2 * seqs * pairs * rows * keys,
        ),
    )(qn, qr, latent, latent, weights, keyval, grad_mixed, log_sum, key_pos, limit, cosines, sines, latents_before, *waits)


def ffn_kernel(pieces, *refs):
    rows_h, rows_g, weight = refs[:pieces], refs[pieces : 2 * pieces], refs[2 * pieces]
    unit_gu, unit_d = refs[2 * pieces + 1], refs[2 * pieces + 2]
    branch, grad_rows = refs[2 * pieces + 3 : 3 * pieces + 3], refs[3 * pieces + 3 : 4 * pieces + 3]
    acts, grad_gate_up, grad_gates, total, grad_total = refs[4 * pieces + 3 :]
    piece = pl.program_id(0)
    step = pl.program_id(1)
    steps = pl.num_programs(1)
    units, hidden, width = unit_d.shape

    def work(source_h, source_g):
        w_gu = unit_gu[...].reshape(2 * units * hidden, width)
        w_d = unit_d[...].reshape(units * hidden, width)
        gate_up = dot(w_gu, source_h[...], NT)
        grad_act = dot(w_d, source_g[...], NT)
        act_parts, grad_parts = [], []
        for k in range(units):
            gate = gate_up[2 * k * hidden : (2 * k + 1) * hidden]
            up = gate_up[(2 * k + 1) * hidden : (2 * k + 2) * hidden]
            part = grad_act[k * hidden : (k + 1) * hidden]
            scale = weight[0, k]
            sigmoid = 1.0 / (1.0 + jnp.exp(-gate))
            silu = gate * sigmoid
            act = silu * up
            grad_gates[0, k] = jnp.sum(act * part, axis=0, keepdims=True)
            act_parts.append((act * scale).astype(narrow))
            part = part * scale
            grad_parts.append((part * up * (sigmoid + silu * (1.0 - sigmoid))).astype(narrow))
            grad_parts.append((part * silu).astype(narrow))
        act_rows = jnp.concatenate(act_parts, axis=0)
        grad_gu = jnp.concatenate(grad_parts, axis=0)
        acts[0] = act_rows.reshape(acts.shape[1:])
        grad_gate_up[0] = grad_gu.reshape(grad_gate_up.shape[1:])
        for first in range(0, width, 1024):
            part = slice(first, first + 1024)
            out = dot(act_rows, w_d[:, part], TN)
            grad = dot(grad_gu, w_gu[:, part], TN)

            @pl.when(step == 0)
            def _(part=part, out=out, grad=grad):
                total[:, part] = out
                grad_total[:, part] = grad

            @pl.when(step > 0)
            def _(part=part, out=out, grad=grad):
                total[:, part] += out
                grad_total[:, part] += grad

    for s in range(pieces):

        @pl.when(piece == s)
        def _(s=s):
            work(rows_h[s], rows_g[s])

            @pl.when(step == steps - 1)
            def _():
                branch[s][...] = total[...].astype(narrow)
                grad_rows[s][...] = grad_total[...].astype(narrow)


def feed_forward(rows_h, rows_g, weights, unit_rows, waits=()):
    pieces = len(rows_h)
    count, width = rows_h[0].shape
    units, hidden, _ = unit_rows.shape
    hidden = hidden // 3
    block = min(units, 4)
    whole = pl.BlockSpec((count, width), lambda s, j: (0, 0), pipeline_mode=pl.Buffered(1))

    def units_of(rows, columns):
        return pl.BlockSpec((1, block, rows, columns), lambda s, j: (s, j, 0, 0))

    outs = pl.pallas_call(
        without(functools.partial(ffn_kernel, pieces), 2 * pieces + 3, waits),
        grid=(pieces, units // block),
        in_specs=[whole] * (2 * pieces)
        + [
            units_of(1, count),
            pl.BlockSpec((block, 2 * hidden, width), lambda s, j: (j, 0, 0)),
            pl.BlockSpec((block, hidden, width), lambda s, j: (j, 2, 0)),
        ]
        + waiting(waits),
        out_specs=[whole] * (2 * pieces)
        + [units_of(hidden, count), units_of(2 * hidden, count), units_of(1, count)],
        out_shape=[jax.ShapeDtypeStruct((count, width), narrow)] * (2 * pieces)
        + [
            jax.ShapeDtypeStruct((pieces, units, hidden, count), narrow),
            jax.ShapeDtypeStruct((pieces, units, 2 * hidden, count), narrow),
            jax.ShapeDtypeStruct((pieces, units, 1, count), wide),
        ],
        scratch_shapes=[pltpu.VMEM((count, width), wide), pltpu.VMEM((count, width), wide)],
        compiler_params=pltpu.CompilerParams(vmem_limit_bytes=60 * 1024 * 1024),
        cost_estimate=pl.CostEstimate(
            flops=12 * pieces * units * hidden * count * width,
            bytes_accessed=pieces * (6 * units * hidden * width + 8 * count * width),
            transcendentals=pieces * units * hidden * count,
        ),
    )(*rows_h, *rows_g, jnp.stack(weights), unit_rows, unit_rows, *waits)
    return [
        (outs[s], outs[pieces + s], outs[2 * pieces], outs[2 * pieces + 1], outs[2 * pieces + 2][s], s)
        for s in range(pieces)
    ]


def weight_grad_kernel(pieces, joined, order, *refs):
    rows_h, rows_g = refs[:pieces], refs[pieces : 2 * pieces]
    acts, grads = refs[2 * pieces : 4 * pieces], refs[4 * pieces : 6 * pieces]
    out = refs[6 * pieces + joined]
    hidden = acts[0].shape[2]
    for k in range(2):
        gate_up = sum(
            dot(grads[2 * s + k][0, 0], rows_h[s][...], NN) for s in range(pieces)
        )
        down = sum(dot(acts[2 * s + k][0, 0], rows_g[s][...], NN) for s in range(pieces))
        if joined:
            before = refs[6 * pieces]
            gate_up += before[k, : 2 * hidden].astype(wide)
            down += before[k, 2 * hidden :].astype(wide)
        out[k, : 2 * hidden] = gate_up.astype(narrow)
        out[k, 2 * hidden :] = down.astype(narrow)


def weight_grads(found, rows_h, rows_g, order, before=None, waits=()):
    pieces, units = len(found), order.shape[0]
    _, _, hidden, count = found[0][2].shape
    width = rows_h[0].shape[1]
    joined = 0 if before is None else 1
    whole = pl.BlockSpec(
        (count, width), lambda j, order: (0, 0), pipeline_mode=pl.Buffered(1)
    )
    pair = pl.BlockSpec((2, 3 * hidden, width), lambda j, order: (j, 0, 0))

    def units_of(rows, at):
        return [
            pl.BlockSpec((1, 1, rows, count), lambda j, order, k=k: (at, order[2 * j + k], 0, 0))
            for k in range(2)
        ]

    return pl.pallas_call(
        without(
            functools.partial(weight_grad_kernel, pieces, joined), 6 * pieces + joined + 1, waits
        ),
        grid_spec=pltpu.PrefetchScalarGridSpec(
            num_scalar_prefetch=1,
            grid=(units // 2,),
            in_specs=[whole] * (2 * pieces)
            + [spec for item in found for spec in units_of(hidden, item[5])]
            + [spec for item in found for spec in units_of(2 * hidden, item[5])]
            + [pair] * joined
            + waiting(waits),
            out_specs=pair,
        ),
        out_shape=jax.ShapeDtypeStruct((units, 3 * hidden, width), narrow),
        compiler_params=pltpu.CompilerParams(vmem_limit_bytes=60 * 1024 * 1024),
        cost_estimate=pl.CostEstimate(
            flops=6 * pieces * units * hidden * count * width,
            bytes_accessed=6 * units * hidden * (width + pieces * count)
            + 4 * pieces * count * width,
            transcendentals=0,
        ),
    )(
        order,
        *rows_h,
        *rows_g,
        *[item[2] for item in found for _ in range(2)],
        *[item[3] for item in found for _ in range(2)],
        *([] if before is None else [before]),
        *waits,
    )


def zero_of(*others):
    firsts = [lax.slice(o, [0] * o.ndim, [1] * o.ndim).reshape(()) for o in others]
    return sum(jnp.where(first != first, 1.0, 0.0) for first in firsts)


def after(values, *others):
    if not others:
        return values
    return (values.astype(wide) + zero_of(*others)).astype(values.dtype)


def hop(values):
    count = lax.axis_size("tp")
    return lax.ppermute(values, "tp", [(i, (i + 1) % count) for i in range(count)])


def ring_gather(values):
    pieces = [values]
    for _ in range(lax.axis_size("tp") - 1):
        pieces.append(hop(pieces[-1]))
    return pieces


def ring_scatter(pieces):
    total = pieces[1].astype(narrow)
    for piece in pieces[2:]:
        total = (hop(total).astype(wide) + piece).astype(narrow)
    return hop(total).astype(wide) + pieces[0]


def cross_scatter(pieces):
    return sum((item.astype(wide) for item in cross_moves(pieces)), pieces[0].astype(wide))


def scatter_tp(values, axis, rows):
    count, rank = lax.axis_size("tp"), lax.axis_index("tp")
    size = values.shape[axis] // count
    placed = jnp.concatenate(
        [
            lax.dynamic_slice_in_dim(
                values, (rank + count - d) % count * size, size, axis
            ).reshape(rows, -1)
            for d in range(count)
        ],
        axis=0,
    )
    return lax.psum_scatter(placed, "tp", scatter_dimension=0, tiled=True).astype(wide)


def cross_moves(pieces):
    count = lax.axis_size("tp")
    return [
        lax.ppermute(pieces[s].astype(narrow), "tp", [(i, (i - s) % count) for i in range(count)])
        for s in range(1, count)
    ]


def cross_sum(values):
    count, rank = lax.axis_size("tp"), lax.axis_index("tp")
    values = values.astype(narrow)
    pieces = [values] + [
        lax.ppermute(values, "tp", [(i, (i + s) % count) for i in range(count)])
        for s in range(1, count)
    ]
    stacked = jnp.stack(pieces)
    return sum(
        lax.dynamic_index_in_dim(stacked, (rank + count - r) % count, 0, False).astype(wide)
        for r in range(count)
    )


def swap(values, mask):
    return lax.ppermute(values, "fsdp", [(i, i ^ mask) for i in range(lax.axis_size("fsdp"))])


def gather_fsdp(values, axis=0):
    return lax.all_gather(values, "fsdp", axis=axis, tiled=True)


def scatter_fsdp(values, axis=0):
    return lax.psum_scatter(values.astype(narrow), "fsdp", scatter_dimension=axis, tiled=True)


def relative_masks(count):
    return [0, 2, 6, 4] if count == 8 else list(range(0, count, 2))


def relative_blocks(values, other, axis):
    count, rank = lax.axis_size("fsdp"), lax.axis_index("fsdp")
    size = values.shape[axis] // count
    return [
        lax.dynamic_slice_in_dim(values, (rank ^ (mask + other)) * size, size, axis)
        for mask in relative_masks(count)
    ]


class Scatter:
    def __init__(self, sent):
        self.sent = sent.astype(narrow)
        self.received = swap(self.sent, 1)

    def join(self, make, *others):
        part = make(self.received, zero_of(*others) if others else None)
        half = part.shape[1] // 2
        self.part = part
        self.from_x, self.from_y = swap(part[1:3, :half], 2), swap(part[2:4, half:], 4)

    def turn(self, *others):
        half = self.part.shape[1] // 2
        zero = zero_of(*others) if others else 0.0
        self.own_top = self.part[0, :half].astype(wide) + self.from_x[0]
        self.own_low = self.part[0, half:].astype(wide) + self.from_y[1]
        top = (self.part[3, :half].astype(wide) + self.from_x[1] + zero).astype(narrow)
        low = (self.part[1, half:].astype(wide) + self.from_y[0] + zero).astype(narrow)
        self.turned = top
        self.last_top, self.last_low = swap(top, 4), swap(low, 2)

    def end(self, *others):
        zero = zero_of(*others) if others else 0.0
        return jnp.concatenate(
            [self.own_top + self.last_top + zero, self.own_low + self.last_low + zero], axis=0
        )


class WholeScatter:
    def __init__(self, values, axis):
        self.sent = self.part = self.turned = values.astype(narrow)
        self.axis = axis

    def join(self, make, *others):
        pass

    def turn(self, *others):
        pass

    def end(self, *others):
        total = scatter_fsdp(self.sent, self.axis).astype(wide)
        return total + zero_of(*others) if others else total


def joiner(make):
    def join(received, zero):
        total = make(0) + received.astype(wide)
        return (total if zero is None else total + zero).astype(narrow)

    return join


def scatter_product(rows, columns, joined=None):
    count = lax.axis_size("fsdp")
    if count != 8:
        out = dot(rows, columns, TN, narrow)
        if joined is not None:
            out = jnp.concatenate([out, joined.astype(narrow)], axis=1)
        return WholeScatter(out, 0), None

    def make(other):
        chosen = jnp.concatenate(relative_blocks(rows, other, 1), axis=1)
        return dot(chosen, columns, TN).reshape(count // 2, -1, columns.shape[1])

    def more(other):
        return jnp.stack(relative_blocks(joined, other, 0))

    if joined is None:
        return Scatter(make(1)), joiner(make)

    def join(received, zero):
        cut = columns.shape[1]
        zero = 0.0 if zero is None else zero
        return jnp.concatenate(
            [
                (make(0) + received[..., :cut].astype(wide) + zero).astype(narrow),
                (more(0) + received[..., cut:].astype(wide)).astype(narrow),
            ],
            axis=2,
        )

    return Scatter(jnp.concatenate([make(1).astype(narrow), more(1).astype(narrow)], axis=2)), join


def scatter_values(values, axis):
    if lax.axis_size("fsdp") != 8:
        return WholeScatter(values, axis), None

    def make(other):
        return jnp.stack(relative_blocks(values, other, axis))

    return Scatter(make(1)), joiner(make)


def on_device(
    tokens,
    lengths,
    routes,
    slot_ranks,
    attn_gain,
    query_weight,
    latent_key_weight,
    latent_gain,
    kvb_weight,
    output_weight,
    ffn_gain,
    router_matrix,
    shared_gate_weight,
    shared_up_weight,
    shared_down_weight,
    expert_gate,
    expert_up,
    expert_down,
    cotangent,
):
    tp_count = lax.axis_size("tp")
    tp_rank = lax.axis_index("tp")
    fsdp_count = lax.axis_size("fsdp")
    seq_count, local_len, width = tokens.shape
    seq_len = local_len * tp_count
    group_rows = seq_count * seq_len
    own_rows = seq_count * local_len
    own_experts = expert_gate.shape[0]
    expert_count = own_experts * fsdp_count
    capacity = 4 * group_rows // expert_count
    ffe = expert_gate.shape[2]
    sff = shared_gate_weight.shape[1]
    head_local = HEAD_COUNT // tp_count
    own_first = tp_rank * local_len
    own_positions = own_first + jnp.arange(local_len, dtype=jnp.int32)
    rel_rank = [(tp_rank + tp_count - s) % tp_count for s in range(tp_count)]
    key_pos = jnp.concatenate(
        [r * local_len + jnp.arange(local_len, dtype=jnp.int32) for r in rel_rank]
    )
    limit = jnp.minimum(own_positions[None, :], lengths[:, None] - 1)[..., None]

    shard = attn_gain.shape[0]
    latent_shard = latent_gain.shape[0]
    latent_width = latent_key_weight.shape[1]
    gain_rows = [latent_width, latent_width + 8, latent_width + 16]
    router_first = latent_width + 24
    small_rows = -(-(router_first + expert_count) // 32) * 32

    def small_stack(latent_key, attn, ffn, latent, router):
        rows = [latent_key]
        for gain in (attn, ffn, latent):
            rows.append(jnp.pad(gain[None], ((0, 7), (0, 0))))
        rows += [router]
        if small_rows > router_first + expert_count:
            rows.append(
                jnp.zeros((small_rows - router_first - expert_count, router.shape[1]), router.dtype)
            )
        return jnp.concatenate(rows, axis=0)

    small_shard = small_stack(
        latent_key_weight.T,
        attn_gain,
        ffn_gain,
        jnp.pad(latent_gain, (0, shard - latent_shard)),
        router_matrix.T,
    )
    small_all = gather_fsdp(small_shard, axis=1)
    latent_key_whole = small_all[:latent_width]
    attn_scale = small_all[gain_rows[0]].astype(wide)
    ffn_scale = small_all[gain_rows[1]].astype(wide)
    latent_scale = (
        small_all[gain_rows[2]]
        .reshape(fsdp_count, shard)[:, :latent_shard]
        .reshape(-1)
        .astype(wide)
    )
    router_t = small_all[router_first : router_first + expert_count]

    query_heads = query_weight.reshape(shard, head_local, PLAIN_WIDTH + ROTARY_WIDTH)
    nope_cols, rope_cols = head_local * PLAIN_WIDTH, head_local * ROTARY_WIDTH
    query_cols, output_cols = query_weight.shape[1], output_weight.shape[0]
    kv_rows, kv_cols = kvb_weight.shape
    quarters = shard // kv_rows
    kvb_columns = kv_cols // quarters
    attention_shard = jnp.concatenate(
        [
            query_heads[..., :PLAIN_WIDTH].reshape(shard, -1),
            query_heads[..., PLAIN_WIDTH:].reshape(shard, -1),
            output_weight.T,
            jnp.concatenate(jnp.split(kvb_weight, quarters, axis=1), axis=0),
        ],
        axis=1,
    )
    attention_pieces = ring_gather(after(attention_shard, small_shard))
    cuts = [0, nope_cols, query_cols, query_cols + output_cols, query_cols + output_cols + kvb_columns]
    attention_joined = jnp.concatenate(
        [
            piece[:, first:last]
            for first, last in zip(cuts[:-1], cuts[1:])
            for piece in attention_pieces
        ],
        axis=1,
    )
    attention_all = gather_fsdp(attention_joined)
    query_end = tp_count * query_cols
    kvb_first = query_end + tp_count * output_cols
    query_whole = attention_all[:, :query_end]
    output_whole = attention_all[:, query_end:kvb_first]
    kvb_whole = attention_all.reshape(fsdp_count, quarters, kv_rows, -1)

    token_rows = tokens.reshape(own_rows, width).astype(wide)
    normed = normalize(token_rows, attn_scale).astype(narrow)
    latent_rows = dot(normed, latent_key_whole, NT)
    compressed = latent_rows[:, :RANK]
    compressed_n = normalize(compressed, latent_scale).astype(narrow)
    row_positions = jnp.concatenate([own_positions] * seq_count)
    key_rope_own = rotate(latent_rows[:, RANK:], row_positions, 1.0).astype(narrow)
    latent_pieces = ring_gather(
        after(
            jnp.concatenate([compressed_n, key_rope_own, key_rope_own], axis=1),
            attention_joined,
        )
    )
    latent_all = jnp.concatenate(
        [piece.reshape(seq_count, local_len, -1) for piece in latent_pieces], axis=1
    )

    split = 2 if ffe % 32 == 0 else 1
    unit = ffe // split
    shared_units = sff // unit
    shared_shard = jnp.concatenate(
        [
            shared_gate_weight.T.reshape(shared_units, unit, shard),
            shared_up_weight.T.reshape(shared_units, unit, shard),
            shared_down_weight.reshape(shared_units, unit, shard),
        ],
        axis=1,
    )
    weights = [
        gather_fsdp(after(shared_shard.reshape(3 * sff, shard), latent_pieces[2]), axis=1).reshape(
            shared_units, 3 * unit, width
        )
    ]
    gate_rows, up_rows = expert_gate[0].T, expert_up[0].T
    for g in range(split):
        part = slice(g * unit, (g + 1) * unit)
        shard_rows = jnp.concatenate([gate_rows[part], up_rows[part], expert_down[0, part]], axis=0)
        weights.append(
            gather_fsdp(after(shard_rows, latent_pieces[1 + 2 * g])).reshape(
                expert_count, 3 * unit, width
            )
        )

    live_mask = (own_positions[None, :] < lengths[:, None]).astype(wide).reshape(own_rows, 1)
    grad_out = live_mask * cotangent.reshape(own_rows, width).astype(wide)
    grad_pieces = ring_gather(after(grad_out.astype(narrow), latent_all))

    cosines, sines = rotary_tables(own_positions, 128)
    query_nope, query_rope = project(
        normed,
        attention_all,
        jnp.concatenate([cosines] * seq_count),
        jnp.concatenate([sines] * seq_count),
    )
    query_nope = query_nope.reshape(seq_count, local_len, -1)
    query_rope = query_rope.reshape(seq_count, local_len, -1)
    key_row = key_pos[None, :]
    mixed, log_sums, keyval = attend(
        query_nope, query_rope, latent_all, kvb_whole, kvb_first, kvb_columns,
        key_row, limit
    )
    mixed = mixed.reshape(own_rows, -1)
    hidden = token_rows + dot(mixed, output_whole, NT)
    hidden_normed = normalize(hidden, ffn_scale).astype(narrow)
    hidden_pieces = ring_gather(hidden_normed)

    expert_ids = jnp.arange(expert_count, dtype=jnp.int32)[:, None, None]
    ones = jnp.ones((shared_units, 1, own_rows), wide)
    gate_tables = []
    for s in range(tp_count):
        first = rel_rank[s] * local_len
        route_t = lax.dynamic_slice_in_dim(routes, first, local_len, 1).reshape(own_rows, TOPK).T
        rank_t = lax.dynamic_slice_in_dim(slot_ranks, first, local_len, 1).reshape(own_rows, TOPK).T
        hits = route_t[None] == expert_ids
        chosen = jnp.any(hits, axis=1)
        kept = jnp.any(hits & (rank_t < capacity)[None], axis=1).astype(wide)
        logits = dot(router_t, hidden_pieces[s], NT)
        picked = jnp.where(chosen, logits, -1e30)
        exponent = jnp.where(chosen, jnp.exp(picked - jnp.max(picked, axis=0, keepdims=True)), 0.0)
        gates = exponent / jnp.sum(exponent, axis=0, keepdims=True)
        gate_tables.append((gates, kept))

    chunks = range(tp_count)
    results = {}
    previous = []

    def run(group, which, *waits):
        tables = [
            ones if group == 0 else (gate_tables[s][0] * gate_tables[s][1])[:, None, :]
            for s in which
        ]
        found = feed_forward(
            [hidden_pieces[s] for s in which],
            [grad_pieces[s] for s in which],
            tables,
            weights[group],
            [*previous, *waits],
        )
        for s, item in zip(which, found):
            results[group, s] = item
        previous[:] = [found[0][4]]

    def grads_of(group, units, *others, before=None):
        out = weight_grads(
            [results[group, s] for s in chunks],
            hidden_pieces,
            grad_pieces,
            units,
            before,
            [*previous, *others],
        )
        previous[:] = [out]
        return out

    def finish_piece(s, *others):
        found = [results[g, s] for g in range(split + 1)]
        branch = sum(item[0].astype(wide) for item in found).astype(narrow)
        gates, kept = gate_tables[s]
        grad_gates = sum(item[4][:, 0] for item in found[1:]) * kept
        logits = (
            gates * (grad_gates - jnp.sum(gates * grad_gates, axis=0, keepdims=True))
        ).astype(narrow)
        grad_hidden = sum(item[1].astype(wide) for item in found)
        if others:
            grad_hidden += zero_of(*others)
        return branch, grad_hidden + dot(logits, router_t, TN), logits

    last_order = list(chunks[1:]) + [0]
    pairs = [chunks[s : s + 2] for s in range(0, tp_count, 2)]
    if split == 2:
        run(1, [0])
        run(1, [1])
    run(0, [0])
    run(0, [1], hidden_pieces[2])
    for which in pairs[1:]:
        if split == 2:
            for s in which:
                run(1, [s])
        run(0, which)
    all_units = jnp.arange(expert_count, dtype=jnp.int32)
    shared_sum = scatter_fsdp(
        grads_of(0, jnp.arange(shared_units, dtype=jnp.int32)).reshape(3 * sff, width), 1
    )
    first_sum = None
    if split == 2:
        first_sum = scatter_fsdp(grads_of(1, all_units).reshape(-1, width))

    pieces, total = {}, None
    for k, s in enumerate(last_order):
        if k == 2:
            previous.append(shared_sum)
            branch_total = after(pieces[last_order[0]][0], *previous)
            previous.append(branch_total)
        if k == tp_count - 1:
            pieces[last_order[1]] = finish_piece(last_order[1], *previous)
            total = (hop(total).astype(wide) + pieces[last_order[1]][1]).astype(narrow)
            branch_total = (
                hop(branch_total).astype(wide) + after(pieces[last_order[1]][0], total)
            ).astype(narrow)
            previous += [total, branch_total]
        run(split, [s])
        if k == 0:
            pieces[s] = finish_piece(s)
            total = pieces[s][1].astype(narrow)
            previous.append(total)
    for s in last_order[2:-1]:
        pieces[s] = finish_piece(s, *previous)
        total = (hop(total).astype(wide) + pieces[s][1]).astype(narrow)
    previous.append(total)
    if first_sum is not None:
        previous.append(first_sum)
    last_sum = scatter_fsdp(grads_of(split, all_units).reshape(-1, width))
    pieces[0] = finish_piece(0, *previous)
    grad_hidden_own = hop(total).astype(wide) + pieces[0][1]

    hidden_back = jax.vjp(normalize, hidden, ffn_scale)[1]
    grad_hnorm, grad_ffn_gain = hidden_back(grad_hidden_own)
    grad_hidden = grad_out + grad_hnorm
    grad_attn = grad_hidden.astype(narrow)
    branch_total = after(branch_total, grad_attn)
    out_scatter, make_out = scatter_product(grad_attn, mixed)
    grad_mixed = dot(grad_attn, output_whole, NN, narrow)

    def back(first, pairs, rows, latents_before, waits):
        return attend_back(
            query_nope, query_rope, latent_all, kvb_whole, kvb_first, kvb_columns, keyval,
            rows.reshape(seq_count, local_len, -1), log_sums, key_row, limit,
            cosines, sines, latents_before, first, pairs, waits,
        )

    pairs_half = HEAD_COUNT // 4
    first_qn, first_qr, first_latents, first_kvb = back(
        0, pairs_half, grad_mixed, jnp.zeros_like(latent_all), [out_scatter.sent, branch_total]
    )
    first_query = jnp.concatenate([first_qn, first_qr], axis=-1).reshape(own_rows, -1)
    first_scatter, make_first_query = scatter_product(
        normed, first_query, first_kvb.reshape(width, -1)
    )
    out_scatter.join(make_out, first_scatter.sent)
    for s in last_order[2:-1]:
        branch_total = (
            hop(branch_total).astype(wide) + after(pieces[s][0], out_scatter.part)
        ).astype(narrow)
    second_qn, second_qr, grad_latent_all, second_kvb = back(
        pairs_half, pairs_half, grad_mixed, first_latents,
        [branch_total, out_scatter.part, last_sum],
    )

    grad_latent_sum = scatter_tp(grad_latent_all, 1, own_rows)
    second_query = jnp.concatenate([second_qn, second_qr], axis=-1).reshape(own_rows, -1)
    second_scatter, make_second_query = scatter_product(
        normed, second_query, second_kvb.reshape(width, -1)
    )
    out_scatter.turn(second_scatter.sent)
    branch_moved = hop(branch_total)
    first_scatter.join(make_first_query, out_scatter.turned, branch_moved)
    second_scatter.join(make_second_query, first_scatter.part)
    half_plain, half_turned = first_qn.shape[2], first_qr.shape[2]
    router_gradient = sum(
        dot(after(pieces[s][2], second_scatter.part), hidden_pieces[s], NN) for s in chunks
    )
    query_gradient = jnp.concatenate(
        [
            first_query[:, :half_plain],
            second_query[:, :half_plain],
            first_query[:, half_plain:],
            second_query[:, half_plain:],
        ],
        axis=1,
    )
    grad_normed = dot(after(query_gradient, second_scatter.part, grad_latent_sum), query_whole, NT)
    first_scatter.turn(grad_normed)

    latent_back = jax.vjp(normalize, compressed, latent_scale)[1]
    grad_compressed, grad_latent_gain = latent_back(grad_latent_sum[:, :RANK])
    latent_gradient = jnp.concatenate(
        [
            grad_compressed,
            rotate(grad_latent_sum[:, RANK : RANK + ROTARY_WIDTH], row_positions, -1.0),
        ],
        axis=-1,
    ).astype(narrow)
    latent_key_gradient = dot(latent_gradient, normed, TN)
    grad_normed = grad_normed + dot(latent_gradient, latent_key_whole, NN)
    token_back = jax.vjp(normalize, token_rows, attn_scale)[1]
    grad_tnorm, grad_attn_gain = token_back(grad_normed)
    grad_tokens = (grad_hidden + grad_tnorm).astype(narrow).reshape(tokens.shape)


    small_grads = small_stack(
        latent_key_gradient,
        grad_attn_gain,
        grad_ffn_gain,
        jnp.pad(
            grad_latent_gain.reshape(fsdp_count, latent_shard),
            ((0, 0), (0, shard - latent_shard)),
        ).reshape(-1),
        router_gradient,
    )
    small_sum = cross_sum(scatter_fsdp(small_grads, 1))
    second_scatter.turn(small_grads)

    out_sum = out_scatter.end(small_grads)
    first_own = first_scatter.end()
    second_own = second_scatter.end()
    half_query = half_plain + half_turned

    def query_piece(s):
        half = tp_count // 2
        values, at = (first_own, s) if s < half else (second_own, s - half)
        return jnp.concatenate(
            [
                values[:, at * nope_cols : (at + 1) * nope_cols],
                values[:, half_plain + at * rope_cols : half_plain + (at + 1) * rope_cols],
                values[:, half_query + at * kvb_columns : half_query + (at + 1) * kvb_columns],
            ],
            axis=1,
        )

    out_own = cross_scatter(jnp.split(out_sum, tp_count, axis=1)).T
    query_own = cross_scatter([query_piece(s) for s in chunks])
    branch_own = branch_moved.astype(wide) + after(pieces[0][0], small_grads)
    output = (live_mask * (hidden + branch_own)).astype(narrow).reshape(tokens.shape)
    kvb_own = jnp.concatenate(jnp.split(query_own[:, query_cols:], quarters, axis=0), axis=1)
    query_own = jnp.concatenate(
        [
            query_own[:, :nope_cols].reshape(shard, head_local, PLAIN_WIDTH),
            query_own[:, nope_cols:query_cols].reshape(shard, head_local, ROTARY_WIDTH),
        ],
        axis=-1,
    ).reshape(shard, -1)
    shared_sum = shared_sum.astype(wide).reshape(shared_units, 3, unit, shard)
    expert_sum = [last_sum] if first_sum is None else [first_sum, last_sum]
    expert_sum = jnp.concatenate(
        [item.astype(wide).reshape(3, unit, width) for item in expert_sum], axis=1
    )
    return (
        output,
        grad_tokens,
        small_sum[gain_rows[0]],
        query_own,
        small_sum[:latent_width].T,
        small_sum[gain_rows[2], :latent_shard],
        kvb_own,
        out_own,
        small_sum[gain_rows[1]],
        small_sum[router_first : router_first + expert_count].T,
        shared_sum[:, 0].reshape(sff, shard).T,
        shared_sum[:, 1].reshape(sff, shard).T,
        shared_sum[:, 2].reshape(sff, shard),
        expert_sum[0].T[None],
        expert_sum[1].T[None],
        expert_sum[2][None],
    )


def solution(mesh):
    in_specs = (
        P("fsdp", "tp", None),
        P("fsdp"),
        P("fsdp", None, None),
        P("fsdp", None, None),
        P("fsdp"),
        P("fsdp", "tp"),
        P("fsdp", None),
        P("fsdp"),
        P("fsdp", "tp"),
        P("tp", "fsdp"),
        P("fsdp"),
        P("fsdp", None),
        P("fsdp", "tp"),
        P("fsdp", "tp"),
        P("tp", "fsdp"),
        P("fsdp", None, "tp"),
        P("fsdp", None, "tp"),
        P("fsdp", "tp", None),
        P("fsdp", "tp", None),
    )
    out_specs = (
        P("fsdp", "tp", None),
        P("fsdp", "tp", None),
        P("fsdp"),
        P("fsdp", "tp"),
        P("fsdp", None),
        P("fsdp"),
        P("fsdp", "tp"),
        P("tp", "fsdp"),
        P("fsdp"),
        P("fsdp", None),
        P("fsdp", "tp"),
        P("fsdp", "tp"),
        P("tp", "fsdp"),
        P("fsdp", None, "tp"),
        P("fsdp", None, "tp"),
        P("fsdp", "tp", None),
    )
    return jax.shard_map(
        on_device, mesh=mesh, in_specs=in_specs, out_specs=out_specs, check_vma=False
    )
```

```python
import functools

import jax
import jax.numpy as jnp
from jax import lax
from jax.experimental import pallas as pl
from jax.experimental.pallas import tpu as pltpu
from jax.sharding import PartitionSpec as P

HEAD_COUNT = 16
PLAIN_WIDTH = 128
ROTARY_WIDTH = 64
VALUE_WIDTH = 128
RANK = 512
TOPK = 6
SCALE = (PLAIN_WIDTH + ROTARY_WIDTH) ** (-0.5)

epsilon = 1e-06
narrow = jnp.bfloat16
wide = jnp.float32
VMEM_LIMIT = 48 * 1024 * 1024


def normalize(values, gain_row):
    return (
        values * lax.rsqrt(jnp.mean(values * values, axis=-1, keepdims=True) + epsilon) * gain_row
    )


def rotate(values, positions, direction):
    half_width = values.shape[-1] // 2
    frequency = 10000.0 ** (-jnp.arange(half_width, dtype=wide) / half_width)
    angles = positions.astype(wide)[..., None] * frequency
    cosines = jnp.cos(angles)
    sines = jnp.sin(angles) * direction
    first_half = values[..., :half_width]
    second_half = values[..., half_width:]
    return jnp.concatenate(
        [first_half * cosines - second_half * sines, first_half * sines + second_half * cosines],
        axis=-1,
    )


def dot(a, b, dims, out=wide):
    return lax.dot_general(a, b, (dims, ((), ())), preferred_element_type=wide).astype(out)


NN = ((1,), (0,))
NT = ((1,), (1,))
TN = ((0,), (0,))


def without(kernel, inputs, waits):
    def body(*refs):
        kernel(*refs[:inputs], *refs[inputs + len(waits) :])

    return body


def waiting(waits):
    return [pl.BlockSpec(memory_space=pl.ANY)] * len(waits)


def swap_halves(values):
    lane = lax.broadcasted_iota(jnp.int32, values.shape, 1)
    count, half = values.shape[1], ROTARY_WIDTH // 2
    return jnp.where(
        lane % ROTARY_WIDTH < half,
        pltpu.roll(values, count - half, 1),
        pltpu.roll(values, half, 1),
    )


def rotary_tables(positions, columns):
    half = ROTARY_WIDTH // 2
    frequency = 10000.0 ** (-jnp.arange(half, dtype=wide) / half)
    angles = positions.astype(wide)[:, None] * frequency
    cosines, sines = jnp.cos(angles), jnp.sin(angles)
    repeats = columns // ROTARY_WIDTH
    return (
        jnp.concatenate([cosines, cosines] * repeats, axis=1),
        jnp.concatenate([-sines, sines] * repeats, axis=1),
    )


def project_kernel(rows, weights, cosines, sines, nope, rope):
    step = pl.program_id(0)
    out = dot(rows[...], weights[...], NN)

    @pl.when(step < HEAD_COUNT * PLAIN_WIDTH // 512)
    def _():
        nope[...] = out.astype(narrow)

    @pl.when(step >= HEAD_COUNT * PLAIN_WIDTH // 512)
    def _():
        turned = out * jnp.concatenate([cosines[...]] * 4, axis=1)
        turned += swap_halves(out) * jnp.concatenate([sines[...]] * 4, axis=1)
        rope[...] = turned.astype(narrow)


def project(rows, weights, cosines, sines):
    count, width = rows.shape
    plain = HEAD_COUNT * PLAIN_WIDTH // 512
    turned = HEAD_COUNT * ROTARY_WIDTH // 512
    return pl.pallas_call(
        project_kernel,
        grid=(plain + turned,),
        in_specs=[
            pl.BlockSpec((count, width), lambda j: (0, 0)),
            pl.BlockSpec((width, 512), lambda j: (0, j)),
            pl.BlockSpec((count, 128), lambda j: (0, 0)),
            pl.BlockSpec((count, 128), lambda j: (0, 0)),
        ],
        out_specs=[
            pl.BlockSpec((count, 512), lambda j: (0, jnp.minimum(j, plain - 1))),
            pl.BlockSpec((count, 512), lambda j: (0, jnp.maximum(j - plain, 0))),
        ],
        out_shape=[
            jax.ShapeDtypeStruct((count, 512 * plain), narrow),
            jax.ShapeDtypeStruct((count, 512 * turned), narrow),
        ],
        compiler_params=pltpu.CompilerParams(vmem_limit_bytes=VMEM_LIMIT),
        cost_estimate=pl.CostEstimate(
            flops=2 * count * width * 512 * (plain + turned),
            bytes_accessed=2 * width * 512 * (plain + turned),
            transcendentals=0,
        ),
    )(rows, weights, cosines, sines)


def pair_half(shape, half):
    lane = lax.broadcasted_iota(jnp.int32, shape, len(shape) - 1)
    return (lane // ROTARY_WIDTH) == half


def attend_kernel(qn, qr, latent, rope, kvb, key_pos, limit, mixed, log_sum, keyval):
    kv = dot(latent[0], kvb_block(kvb), NN, narrow)
    keyval[0] = kv
    live = key_pos[...] <= limit[0]
    rope_keys = rope[0]
    for half in range(2):
        lo = half * 256
        keys = jnp.concatenate([kv[:, lo : lo + 128], rope_keys], axis=1)
        rope_rows = jnp.where(pair_half(qr.shape[1:], half), qr[0], jnp.zeros_like(qr[0]))
        queries = jnp.concatenate([qn[0, :, half * 128 : half * 128 + 128], rope_rows], axis=1)
        scores = jnp.where(live, dot(queries, keys, NT) * SCALE, -1e30)
        row_max = jnp.max(scores, axis=-1, keepdims=True)
        exponent = jnp.exp(scores - row_max)
        row_sum = jnp.sum(exponent, axis=-1, keepdims=True)
        chances = (exponent * (1.0 / row_sum)).astype(narrow)
        rows = dot(chances, kv[:, lo + 128 : lo + 256], NN, narrow)
        mixed[0, :, half * 128 : half * 128 + 128] = rows
        log_sum[0, :, half * 128 : half * 128 + 128] = jnp.broadcast_to(
            row_max + jnp.log(row_sum), rows.shape
        )


def kvb_spec(weights, first, columns):
    count, quarters, rows, _ = weights.shape
    per_piece = quarters * columns // 512
    return pl.BlockSpec(
        (count, 512 // columns, rows, columns),
        lambda p, s: (0, p % per_piece, 0, first // columns + p // per_piece),
    )


def kvb_block(kvb):
    return jnp.concatenate(
        [kvb[:, q].reshape(RANK, kvb.shape[3]) for q in range(kvb.shape[1])], axis=1
    )


def attend(qn, qr, latent, weights, kvb_first, kvb_columns, key_pos, limit):
    seqs, rows, width = qn.shape
    keys = latent.shape[1]
    pairs = HEAD_COUNT // 2
    kv_width = HEAD_COUNT * (PLAIN_WIDTH + VALUE_WIDTH)
    return pl.pallas_call(
        attend_kernel,
        grid=(pairs, seqs),
        in_specs=[
            pl.BlockSpec((1, rows, 256), lambda p, s: (s, 0, p)),
            pl.BlockSpec((1, rows, 128), lambda p, s: (s, 0, p)),
            pl.BlockSpec((1, keys, RANK), lambda p, s: (s, 0, 0)),
            pl.BlockSpec((1, keys, 128), lambda p, s: (s, 0, RANK // 128)),
            kvb_spec(weights, kvb_first, kvb_columns),
            pl.BlockSpec((1, keys), lambda p, s: (0, 0)),
            pl.BlockSpec((1, rows, 1), lambda p, s: (s, 0, 0)),
        ],
        out_specs=[
            pl.BlockSpec((1, rows, 256), lambda p, s: (s, 0, p)),
            pl.BlockSpec((1, rows, 256), lambda p, s: (s, 0, p)),
            pl.BlockSpec((1, keys, 512), lambda p, s: (s, 0, p)),
        ],
        out_shape=[
            jax.ShapeDtypeStruct((seqs, rows, width), narrow),
            jax.ShapeDtypeStruct((seqs, rows, width), wide),
            jax.ShapeDtypeStruct((seqs, keys, kv_width), narrow),
        ],
        compiler_params=pltpu.CompilerParams(vmem_limit_bytes=VMEM_LIMIT),
        cost_estimate=pl.CostEstimate(
            flops=2 * seqs * HEAD_COUNT * keys * (RANK * 256 + rows * 384),
            bytes_accessed=2 * seqs * keys * kv_width,
            transcendentals=seqs * HEAD_COUNT * rows * keys,
        ),
    )(qn, qr, latent, latent, weights, key_pos, limit)


def attend_back_kernel(
    qn, qr, latent, rope, kvb, keyval, grad_mixed, log_sum, key_pos, limit,
    cosines, sines, latents_before, grad_qn, grad_qr, grad_latents, grad_kvb, grad_latent, grad_rope,
):
    pair = pl.program_id(0)
    seq = pl.program_id(1)
    kv = keyval[0]
    live = key_pos[...] <= limit[0]
    rope_keys = rope[0]
    grads = []
    rope_queries = []
    rope_total = None
    for half in range(2):
        lo = half * 256
        values = kv[:, lo + 128 : lo + 256]
        keys = jnp.concatenate([kv[:, lo : lo + 128], rope_keys], axis=1)
        rope_rows = jnp.where(pair_half(qr.shape[1:], half), qr[0], jnp.zeros_like(qr[0]))
        queries = jnp.concatenate([qn[0, :, half * 128 : half * 128 + 128], rope_rows], axis=1)
        sums = log_sum[0, :, half * 128 : half * 128 + 1]
        scores = jnp.where(live, dot(queries, keys, NT) * SCALE, -1e30)
        chances = jnp.exp(scores - sums)
        grad_rows = grad_mixed[0, :, half * 128 : half * 128 + 128]
        grad_chances = dot(grad_rows, values, NT)
        inner = jnp.sum(chances * grad_chances, axis=-1, keepdims=True)
        grad_scores = (chances * (grad_chances - inner)).astype(narrow)
        grad_queries = dot(grad_scores, keys, NN) * SCALE
        grad_qn[0, :, half * 128 : half * 128 + 128] = grad_queries[:, :128].astype(narrow)
        rope_queries.append(grad_queries[:, 128:])
        grad_keys = dot(grad_scores, queries, TN) * SCALE
        grad_values = dot(chances.astype(narrow), grad_rows, TN)
        grads += [grad_keys[:, :128].astype(narrow), grad_values.astype(narrow)]
        rope_part = grad_keys[:, 128:]
        rope_total = rope_part if rope_total is None else rope_total + rope_part
    rope_rows = jnp.where(pair_half(qr.shape[1:], 0), rope_queries[0], rope_queries[1])
    rope_rows = rope_rows * cosines[...] - swap_halves(rope_rows) * sines[...]
    grad_qr[0] = rope_rows.astype(narrow)
    grad_keyval = jnp.concatenate(grads, axis=1)
    latent_part = dot(grad_keyval, kvb_block(kvb), NT)
    kvb_part = dot(latent[0], grad_keyval, TN)

    @pl.when(pair == 0)
    def _():
        grad_latent[seq] = latent_part + latents_before[seq, :, :RANK].astype(wide)
        grad_rope[seq] = rope_total + latents_before[seq, :, RANK:].astype(wide)

    @pl.when(pair > 0)
    def _():
        grad_latent[seq] += latent_part
        grad_rope[seq] += rope_total

    @pl.when(pair == pl.num_programs(0) - 1)
    def _():
        grad_latents[seq, :, :RANK] = grad_latent[seq].astype(narrow)
        rope_sum = grad_rope[seq]
        rope_sum = rope_sum + pltpu.roll(rope_sum, ROTARY_WIDTH, 1)
        grad_latents[seq, :, RANK:] = jnp.where(
            pair_half(rope_sum.shape, 0), rope_sum, 0.0
        ).astype(narrow)

    columns = grad_kvb.shape[3]
    for q in range(grad_kvb.shape[1]):
        part = kvb_part[:, q * columns : (q + 1) * columns].reshape(
            grad_kvb.shape[0], grad_kvb.shape[2], columns
        )

        @pl.when(seq == 0)
        def _(q=q, part=part):
            grad_kvb[:, q] = part

        @pl.when(seq > 0)
        def _(q=q, part=part):
            grad_kvb[:, q] += part


def attend_back(
    qn, qr, latent, weights, kvb_first, kvb_columns, keyval, grad_mixed, log_sum, key_pos, limit,
    cosines, sines, latents_before, first, pairs, waits=(),
):
    seqs, rows, _ = qn.shape
    keys = latent.shape[1]
    width = pairs * 256
    kv = kvb_spec(weights, kvb_first, kvb_columns)
    return pl.pallas_call(
        without(attend_back_kernel, 13, waits),
        grid=(pairs, seqs),
        in_specs=[
            pl.BlockSpec((1, rows, 256), lambda p, s: (s, 0, p + first)),
            pl.BlockSpec((1, rows, 128), lambda p, s: (s, 0, p + first)),
            pl.BlockSpec((1, keys, RANK), lambda p, s: (s, 0, 0)),
            pl.BlockSpec((1, keys, 128), lambda p, s: (s, 0, RANK // 128)),
            pl.BlockSpec(kv.block_shape, lambda p, s: kv.index_map(p + first, s)),
            pl.BlockSpec((1, keys, 512), lambda p, s: (s, 0, p + first)),
            pl.BlockSpec((1, rows, 256), lambda p, s: (s, 0, p + first)),
            pl.BlockSpec((1, rows, 256), lambda p, s: (s, 0, p + first)),
            pl.BlockSpec((1, keys), lambda p, s: (0, 0)),
            pl.BlockSpec((1, rows, 1), lambda p, s: (s, 0, 0)),
            pl.BlockSpec((rows, 128), lambda p, s: (0, 0)),
            pl.BlockSpec((rows, 128), lambda p, s: (0, 0)),
            pl.BlockSpec((seqs, keys, RANK + 128), lambda p, s: (0, 0, 0)),
        ]
        + waiting(waits),
        out_specs=[
            pl.BlockSpec((1, rows, 256), lambda p, s: (s, 0, p)),
            pl.BlockSpec((1, rows, 128), lambda p, s: (s, 0, p)),
            pl.BlockSpec((seqs, keys, RANK + 128), lambda p, s: (0, 0, 0)),
            kvb_spec(weights, 0, kvb_columns),
        ],
        out_shape=[
            jax.ShapeDtypeStruct((seqs, rows, width), narrow),
            jax.ShapeDtypeStruct((seqs, rows, width // 2), narrow),
            jax.ShapeDtypeStruct((seqs, keys, RANK + 128), narrow),
            jax.ShapeDtypeStruct(weights.shape[:3] + (pairs * 512 // weights.shape[1],), wide),
        ],
        scratch_shapes=[
            pltpu.VMEM((seqs, keys, RANK), wide),
            pltpu.VMEM((seqs, keys, 128), wide),
        ],
        compiler_params=pltpu.CompilerParams(vmem_limit_bytes=VMEM_LIMIT),
        cost_estimate=pl.CostEstimate(
            flops=4 * seqs * pairs * keys * (2 * RANK * 256 + rows * 1024),
            bytes_accessed=2 * seqs * keys * pairs * 512,
            transcendentals=2 * seqs * pairs * rows * keys,
        ),
    )(qn, qr, latent, latent, weights, keyval, grad_mixed, log_sum, key_pos, limit, cosines, sines, latents_before, *waits)


def ffn_kernel(pieces, *refs):
    rows_h, rows_g, weight = refs[:pieces], refs[pieces : 2 * pieces], refs[2 * pieces]
    unit_gu, unit_d = refs[2 * pieces + 1], refs[2 * pieces + 2]
    branch, grad_rows = refs[2 * pieces + 3 : 3 * pieces + 3], refs[3 * pieces + 3 : 4 * pieces + 3]
    acts, grad_gate_up, grad_gates, total, grad_total = refs[4 * pieces + 3 :]
    piece = pl.program_id(0)
    step = pl.program_id(1)
    steps = pl.num_programs(1)
    units, hidden, width = unit_d.shape

    def work(source_h, source_g):
        w_gu = unit_gu[...].reshape(2 * units * hidden, width)
        w_d = unit_d[...].reshape(units * hidden, width)
        gate_up = dot(w_gu, source_h[...], NT)
        grad_act = dot(w_d, source_g[...], NT)
        act_parts, grad_parts = [], []
        for k in range(units):
            gate = gate_up[2 * k * hidden : (2 * k + 1) * hidden]
            up = gate_up[(2 * k + 1) * hidden : (2 * k + 2) * hidden]
            part = grad_act[k * hidden : (k + 1) * hidden]
            scale = weight[0, k]
            sigmoid = 1.0 / (1.0 + jnp.exp(-gate))
            silu = gate * sigmoid
            act = silu * up
            grad_gates[0, k] = jnp.sum(act * part, axis=0, keepdims=True)
            act_parts.append((act * scale).astype(narrow))
            part = part * scale
            grad_parts.append((part * up * (sigmoid + silu * (1.0 - sigmoid))).astype(narrow))
            grad_parts.append((part * silu).astype(narrow))
        act_rows = jnp.concatenate(act_parts, axis=0)
        grad_gu = jnp.concatenate(grad_parts, axis=0)
        acts[0] = act_rows.reshape(acts.shape[1:])
        grad_gate_up[0] = grad_gu.reshape(grad_gate_up.shape[1:])
        for first in range(0, width, 1024):
            part = slice(first, first + 1024)
            out = dot(act_rows, w_d[:, part], TN)
            grad = dot(grad_gu, w_gu[:, part], TN)

            @pl.when(step == 0)
            def _(part=part, out=out, grad=grad):
                total[:, part] = out
                grad_total[:, part] = grad

            @pl.when(step > 0)
            def _(part=part, out=out, grad=grad):
                total[:, part] += out
                grad_total[:, part] += grad

    for s in range(pieces):

        @pl.when(piece == s)
        def _(s=s):
            work(rows_h[s], rows_g[s])

            @pl.when(step == steps - 1)
            def _():
                branch[s][...] = total[...].astype(narrow)
                grad_rows[s][...] = grad_total[...].astype(narrow)


def feed_forward(rows_h, rows_g, weights, unit_rows, waits=()):
    pieces = len(rows_h)
    count, width = rows_h[0].shape
    units, hidden, _ = unit_rows.shape
    hidden = hidden // 3
    block = min(units, 4)
    whole = pl.BlockSpec((count, width), lambda s, j: (0, 0), pipeline_mode=pl.Buffered(1))

    def units_of(rows, columns):
        return pl.BlockSpec((1, block, rows, columns), lambda s, j: (s, j, 0, 0))

    outs = pl.pallas_call(
        without(functools.partial(ffn_kernel, pieces), 2 * pieces + 3, waits),
        grid=(pieces, units // block),
        in_specs=[whole] * (2 * pieces)
        + [
            units_of(1, count),
            pl.BlockSpec((block, 2 * hidden, width), lambda s, j: (j, 0, 0)),
            pl.BlockSpec((block, hidden, width), lambda s, j: (j, 2, 0)),
        ]
        + waiting(waits),
        out_specs=[whole] * (2 * pieces)
        + [units_of(hidden, count), units_of(2 * hidden, count), units_of(1, count)],
        out_shape=[jax.ShapeDtypeStruct((count, width), narrow)] * (2 * pieces)
        + [
            jax.ShapeDtypeStruct((pieces, units, hidden, count), narrow),
            jax.ShapeDtypeStruct((pieces, units, 2 * hidden, count), narrow),
            jax.ShapeDtypeStruct((pieces, units, 1, count), wide),
        ],
        scratch_shapes=[pltpu.VMEM((count, width), wide), pltpu.VMEM((count, width), wide)],
        compiler_params=pltpu.CompilerParams(vmem_limit_bytes=60 * 1024 * 1024),
        cost_estimate=pl.CostEstimate(
            flops=12 * pieces * units * hidden * count * width,
            bytes_accessed=pieces * (6 * units * hidden * width + 8 * count * width),
            transcendentals=pieces * units * hidden * count,
        ),
    )(*rows_h, *rows_g, jnp.stack(weights), unit_rows, unit_rows, *waits)
    return [
        (outs[s], outs[pieces + s], outs[2 * pieces], outs[2 * pieces + 1], outs[2 * pieces + 2][s], s)
        for s in range(pieces)
    ]


def weight_grad_kernel(pieces, joined, order, *refs):
    rows_h, rows_g = refs[:pieces], refs[pieces : 2 * pieces]
    acts, grads = refs[2 * pieces : 4 * pieces], refs[4 * pieces : 6 * pieces]
    out = refs[6 * pieces + joined]
    hidden = acts[0].shape[2]
    for k in range(2):
        gate_up = sum(
            dot(grads[2 * s + k][0, 0], rows_h[s][...], NN) for s in range(pieces)
        )
        down = sum(dot(acts[2 * s + k][0, 0], rows_g[s][...], NN) for s in range(pieces))
        if joined:
            before = refs[6 * pieces]
            gate_up += before[k, : 2 * hidden].astype(wide)
            down += before[k, 2 * hidden :].astype(wide)
        out[k, : 2 * hidden] = gate_up.astype(narrow)
        out[k, 2 * hidden :] = down.astype(narrow)


def weight_grads(found, rows_h, rows_g, order, before=None, waits=()):
    pieces, units = len(found), order.shape[0]
    _, _, hidden, count = found[0][2].shape
    width = rows_h[0].shape[1]
    joined = 0 if before is None else 1
    whole = pl.BlockSpec(
        (count, width), lambda j, order: (0, 0), pipeline_mode=pl.Buffered(1)
    )
    pair = pl.BlockSpec((2, 3 * hidden, width), lambda j, order: (j, 0, 0))

    def units_of(rows, at):
        return [
            pl.BlockSpec((1, 1, rows, count), lambda j, order, k=k: (at, order[2 * j + k], 0, 0))
            for k in range(2)
        ]

    return pl.pallas_call(
        without(
            functools.partial(weight_grad_kernel, pieces, joined), 6 * pieces + joined + 1, waits
        ),
        grid_spec=pltpu.PrefetchScalarGridSpec(
            num_scalar_prefetch=1,
            grid=(units // 2,),
            in_specs=[whole] * (2 * pieces)
            + [spec for item in found for spec in units_of(hidden, item[5])]
            + [spec for item in found for spec in units_of(2 * hidden, item[5])]
            + [pair] * joined
            + waiting(waits),
            out_specs=pair,
        ),
        out_shape=jax.ShapeDtypeStruct((units, 3 * hidden, width), narrow),
        compiler_params=pltpu.CompilerParams(vmem_limit_bytes=60 * 1024 * 1024),
        cost_estimate=pl.CostEstimate(
            flops=6 * pieces * units * hidden * count * width,
            bytes_accessed=6 * units * hidden * (width + pieces * count)
            + 4 * pieces * count * width,
            transcendentals=0,
        ),
    )(
        order,
        *rows_h,
        *rows_g,
        *[item[2] for item in found for _ in range(2)],
        *[item[3] for item in found for _ in range(2)],
        *([] if before is None else [before]),
        *waits,
    )


def zero_of(*others):
    firsts = [lax.slice(o, [0] * o.ndim, [1] * o.ndim).reshape(()) for o in others]
    return sum(jnp.where(first != first, 1.0, 0.0) for first in firsts)


def after(values, *others):
    if not others:
        return values
    return (values.astype(wide) + zero_of(*others)).astype(values.dtype)


def hop(values):
    count = lax.axis_size("tp")
    return lax.ppermute(values, "tp", [(i, (i + 1) % count) for i in range(count)])


def ring_gather(values):
    pieces = [values]
    for _ in range(lax.axis_size("tp") - 1):
        pieces.append(hop(pieces[-1]))
    return pieces


def ring_scatter(pieces):
    total = pieces[1].astype(narrow)
    for piece in pieces[2:]:
        total = (hop(total).astype(wide) + piece).astype(narrow)
    return hop(total).astype(wide) + pieces[0]


def cross_scatter(pieces):
    return sum((item.astype(wide) for item in cross_moves(pieces)), pieces[0].astype(wide))


def scatter_tp(values, axis, rows):
    count, rank = lax.axis_size("tp"), lax.axis_index("tp")
    size = values.shape[axis] // count
    placed = jnp.concatenate(
        [
            lax.dynamic_slice_in_dim(
                values, (rank + count - d) % count * size, size, axis
            ).reshape(rows, -1)
            for d in range(count)
        ],
        axis=0,
    )
    return lax.psum_scatter(placed, "tp", scatter_dimension=0, tiled=True).astype(wide)


def cross_moves(pieces):
    count = lax.axis_size("tp")
    return [
        lax.ppermute(pieces[s].astype(narrow), "tp", [(i, (i - s) % count) for i in range(count)])
        for s in range(1, count)
    ]


def cross_sum(values):
    count, rank = lax.axis_size("tp"), lax.axis_index("tp")
    values = values.astype(narrow)
    pieces = [values] + [
        lax.ppermute(values, "tp", [(i, (i + s) % count) for i in range(count)])
        for s in range(1, count)
    ]
    stacked = jnp.stack(pieces)
    return sum(
        lax.dynamic_index_in_dim(stacked, (rank + count - r) % count, 0, False).astype(wide)
        for r in range(count)
    )


def swap(values, mask):
    return lax.ppermute(values, "fsdp", [(i, i ^ mask) for i in range(lax.axis_size("fsdp"))])


def gather_fsdp(values, axis=0):
    return lax.all_gather(values, "fsdp", axis=axis, tiled=True)


def scatter_fsdp(values, axis=0):
    return lax.psum_scatter(values.astype(narrow), "fsdp", scatter_dimension=axis, tiled=True)


def relative_masks(count):
    return [0, 2, 6, 4] if count == 8 else list(range(0, count, 2))


def relative_blocks(values, other, axis):
    count, rank = lax.axis_size("fsdp"), lax.axis_index("fsdp")
    size = values.shape[axis] // count
    return [
        lax.dynamic_slice_in_dim(values, (rank ^ (mask + other)) * size, size, axis)
        for mask in relative_masks(count)
    ]


class Scatter:
    def __init__(self, sent):
        self.sent = sent.astype(narrow)
        self.received = swap(self.sent, 1)

    def join(self, make, *others):
        part = make(self.received, zero_of(*others) if others else None)
        half = part.shape[1] // 2
        self.part = part
        self.from_x, self.from_y = swap(part[1:3, :half], 2), swap(part[2:4, half:], 4)

    def turn(self, *others):
        half = self.part.shape[1] // 2
        zero = zero_of(*others) if others else 0.0
        self.own_top = self.part[0, :half].astype(wide) + self.from_x[0]
        self.own_low = self.part[0, half:].astype(wide) + self.from_y[1]
        top = (self.part[3, :half].astype(wide) + self.from_x[1] + zero).astype(narrow)
        low = (self.part[1, half:].astype(wide) + self.from_y[0] + zero).astype(narrow)
        self.turned = top
        self.last_top, self.last_low = swap(top, 4), swap(low, 2)

    def end(self, *others):
        zero = zero_of(*others) if others else 0.0
        return jnp.concatenate(
            [self.own_top + self.last_top + zero, self.own_low + self.last_low + zero], axis=0
        )


class WholeScatter:
    def __init__(self, values, axis):
        self.sent = self.part = self.turned = values.astype(narrow)
        self.axis = axis

    def join(self, make, *others):
        pass

    def turn(self, *others):
        pass

    def end(self, *others):
        total = scatter_fsdp(self.sent, self.axis).astype(wide)
        return total + zero_of(*others) if others else total


def joiner(make):
    def join(received, zero):
        total = make(0) + received.astype(wide)
        return (total if zero is None else total + zero).astype(narrow)

    return join


def scatter_product(rows, columns, joined=None):
    count = lax.axis_size("fsdp")
    if count != 8:
        out = dot(rows, columns, TN, narrow)
        if joined is not None:
            out = jnp.concatenate([out, joined.astype(narrow)], axis=1)
        return WholeScatter(out, 0), None

    def make(other):
        chosen = jnp.concatenate(relative_blocks(rows, other, 1), axis=1)
        return dot(chosen, columns, TN).reshape(count // 2, -1, columns.shape[1])

    def more(other):
        return jnp.stack(relative_blocks(joined, other, 0))

    if joined is None:
        return Scatter(make(1)), joiner(make)

    def join(received, zero):
        cut = columns.shape[1]
        zero = 0.0 if zero is None else zero
        return jnp.concatenate(
            [
                (make(0) + received[..., :cut].astype(wide) + zero).astype(narrow),
                (more(0) + received[..., cut:].astype(wide)).astype(narrow),
            ],
            axis=2,
        )

    return Scatter(jnp.concatenate([make(1).astype(narrow), more(1).astype(narrow)], axis=2)), join


def scatter_values(values, axis):
    if lax.axis_size("fsdp") != 8:
        return WholeScatter(values, axis), None

    def make(other):
        return jnp.stack(relative_blocks(values, other, axis))

    return Scatter(make(1)), joiner(make)


def on_device(
    tokens,
    lengths,
    routes,
    slot_ranks,
    attn_gain,
    query_weight,
    latent_key_weight,
    latent_gain,
    kvb_weight,
    output_weight,
    ffn_gain,
    router_matrix,
    shared_gate_weight,
    shared_up_weight,
    shared_down_weight,
    expert_gate,
    expert_up,
    expert_down,
    cotangent,
):
    tp_count = lax.axis_size("tp")
    tp_rank = lax.axis_index("tp")
    fsdp_count = lax.axis_size("fsdp")
    seq_count, local_len, width = tokens.shape
    seq_len = local_len * tp_count
    group_rows = seq_count * seq_len
    own_rows = seq_count * local_len
    own_experts = expert_gate.shape[0]
    expert_count = own_experts * fsdp_count
    capacity = 4 * group_rows // expert_count
    ffe = expert_gate.shape[2]
    sff = shared_gate_weight.shape[1]
    head_local = HEAD_COUNT // tp_count
    own_first = tp_rank * local_len
    own_positions = own_first + jnp.arange(local_len, dtype=jnp.int32)
    rel_rank = [(tp_rank + tp_count - s) % tp_count for s in range(tp_count)]
    key_pos = jnp.concatenate(
        [r * local_len + jnp.arange(local_len, dtype=jnp.int32) for r in rel_rank]
    )
    limit = jnp.minimum(own_positions[None, :], lengths[:, None] - 1)[..., None]

    shard = attn_gain.shape[0]
    latent_shard = latent_gain.shape[0]
    latent_width = latent_key_weight.shape[1]
    gain_rows = [latent_width, latent_width + 8, latent_width + 16]
    router_first = latent_width + 24
    small_rows = -(-(router_first + expert_count) // 32) * 32

    def small_stack(latent_key, attn, ffn, latent, router):
        rows = [latent_key]
        for gain in (attn, ffn, latent):
            rows.append(jnp.pad(gain[None], ((0, 7), (0, 0))))
        rows += [router]
        if small_rows > router_first + expert_count:
            rows.append(
                jnp.zeros((small_rows - router_first - expert_count, router.shape[1]), router.dtype)
            )
        return jnp.concatenate(rows, axis=0)

    small_shard = small_stack(
        latent_key_weight.T,
        attn_gain,
        ffn_gain,
        jnp.pad(latent_gain, (0, shard - latent_shard)),
        router_matrix.T,
    )
    small_all = gather_fsdp(small_shard, axis=1)
    latent_key_whole = small_all[:latent_width]
    attn_scale = small_all[gain_rows[0]].astype(wide)
    ffn_scale = small_all[gain_rows[1]].astype(wide)
    latent_scale = (
        small_all[gain_rows[2]]
        .reshape(fsdp_count, shard)[:, :latent_shard]
        .reshape(-1)
        .astype(wide)
    )
    router_t = small_all[router_first : router_first + expert_count]

    query_heads = query_weight.reshape(shard, head_local, PLAIN_WIDTH + ROTARY_WIDTH)
    nope_cols, rope_cols = head_local * PLAIN_WIDTH, head_local * ROTARY_WIDTH
    query_cols, output_cols = query_weight.shape[1], output_weight.shape[0]
    kv_rows, kv_cols = kvb_weight.shape
    quarters = shard // kv_rows
    kvb_columns = kv_cols // quarters
    attention_shard = jnp.concatenate(
        [
            query_heads[..., :PLAIN_WIDTH].reshape(shard, -1),
            query_heads[..., PLAIN_WIDTH:].reshape(shard, -1),
            output_weight.T,
            jnp.concatenate(jnp.split(kvb_weight, quarters, axis=1), axis=0),
        ],
        axis=1,
    )
    attention_pieces = ring_gather(after(attention_shard, small_shard))
    cuts = [0, nope_cols, query_cols, query_cols + output_cols, query_cols + output_cols + kvb_columns]
    attention_joined = jnp.concatenate(
        [
            piece[:, first:last]
            for first, last in zip(cuts[:-1], cuts[1:])
            for piece in attention_pieces
        ],
        axis=1,
    )
    attention_all = gather_fsdp(attention_joined)
    query_end = tp_count * query_cols
    kvb_first = query_end + tp_count * output_cols
    query_whole = attention_all[:, :query_end]
    output_whole = attention_all[:, query_end:kvb_first]
    kvb_whole = attention_all.reshape(fsdp_count, quarters, kv_rows, -1)

    token_rows = tokens.reshape(own_rows, width).astype(wide)
    normed = normalize(token_rows, attn_scale).astype(narrow)
    latent_rows = dot(normed, latent_key_whole, NT)
    compressed = latent_rows[:, :RANK]
    compressed_n = normalize(compressed, latent_scale).astype(narrow)
    row_positions = jnp.concatenate([own_positions] * seq_count)
    key_rope_own = rotate(latent_rows[:, RANK:], row_positions, 1.0).astype(narrow)
    latent_pieces = ring_gather(
        after(
            jnp.concatenate([compressed_n, key_rope_own, key_rope_own], axis=1),
            attention_joined,
        )
    )
    latent_all = jnp.concatenate(
        [piece.reshape(seq_count, local_len, -1) for piece in latent_pieces], axis=1
    )

    split = 2 if ffe % 32 == 0 else 1
    unit = ffe // split
    shared_units = sff // unit
    shared_shard = jnp.concatenate(
        [
            shared_gate_weight.T.reshape(shared_units, unit, shard),
            shared_up_weight.T.reshape(shared_units, unit, shard),
            shared_down_weight.reshape(shared_units, unit, shard),
        ],
        axis=1,
    )
    weights = [
        gather_fsdp(after(shared_shard.reshape(3 * sff, shard), latent_pieces[2]), axis=1).reshape(
            shared_units, 3 * unit, width
        )
    ]
    gate_rows, up_rows = expert_gate[0].T, expert_up[0].T
    for g in range(split):
        part = slice(g * unit, (g + 1) * unit)
        shard_rows = jnp.concatenate([gate_rows[part], up_rows[part], expert_down[0, part]], axis=0)
        weights.append(
            gather_fsdp(after(shard_rows, latent_pieces[1 + 2 * g])).reshape(
                expert_count, 3 * unit, width
            )
        )

    live_mask = (own_positions[None, :] < lengths[:, None]).astype(wide).reshape(own_rows, 1)
    grad_out = live_mask * cotangent.reshape(own_rows, width).astype(wide)
    grad_pieces = ring_gather(after(grad_out.astype(narrow), latent_all))

    cosines, sines = rotary_tables(own_positions, 128)
    query_nope, query_rope = project(
        normed,
        attention_all,
        jnp.concatenate([cosines] * seq_count),
        jnp.concatenate([sines] * seq_count),
    )
    query_nope = query_nope.reshape(seq_count, local_len, -1)
    query_rope = query_rope.reshape(seq_count, local_len, -1)
    key_row = key_pos[None, :]
    mixed, log_sums, keyval = attend(
        query_nope, query_rope, latent_all, kvb_whole, kvb_first, kvb_columns,
        key_row, limit
    )
    mixed = mixed.reshape(own_rows, -1)
    hidden = token_rows + dot(mixed, output_whole, NT)
    hidden_normed = normalize(hidden, ffn_scale).astype(narrow)
    hidden_pieces = ring_gather(hidden_normed)

    expert_ids = jnp.arange(expert_count, dtype=jnp.int32)[:, None, None]
    ones = jnp.ones((shared_units, 1, own_rows), wide)
    gate_tables = []
    for s in range(tp_count):
        first = rel_rank[s] * local_len
        route_t = lax.dynamic_slice_in_dim(routes, first, local_len, 1).reshape(own_rows, TOPK).T
        rank_t = lax.dynamic_slice_in_dim(slot_ranks, first, local_len, 1).reshape(own_rows, TOPK).T
        hits = route_t[None] == expert_ids
        chosen = jnp.any(hits, axis=1)
        kept = jnp.any(hits & (rank_t < capacity)[None], axis=1).astype(wide)
        logits = dot(router_t, hidden_pieces[s], NT)
        picked = jnp.where(chosen, logits, -1e30)
        exponent = jnp.where(chosen, jnp.exp(picked - jnp.max(picked, axis=0, keepdims=True)), 0.0)
        gates = exponent / jnp.sum(exponent, axis=0, keepdims=True)
        gate_tables.append((gates, kept))

    chunks = range(tp_count)
    results = {}
    previous = []

    def run(group, which, *waits):
        tables = [
            ones if group == 0 else (gate_tables[s][0] * gate_tables[s][1])[:, None, :]
            for s in which
        ]
        found = feed_forward(
            [hidden_pieces[s] for s in which],
            [grad_pieces[s] for s in which],
            tables,
            weights[group],
            [*previous, *waits],
        )
        for s, item in zip(which, found):
            results[group, s] = item
        previous[:] = [found[0][4]]

    def grads_of(group, units, *others, before=None):
        out = weight_grads(
            [results[group, s] for s in chunks],
            hidden_pieces,
            grad_pieces,
            units,
            before,
            [*previous, *others],
        )
        previous[:] = [out]
        return out

    def finish_piece(s, *others):
        found = [results[g, s] for g in range(split + 1)]
        branch = sum(item[0].astype(wide) for item in found).astype(narrow)
        gates, kept = gate_tables[s]
        grad_gates = sum(item[4][:, 0] for item in found[1:]) * kept
        logits = (
            gates * (grad_gates - jnp.sum(gates * grad_gates, axis=0, keepdims=True))
        ).astype(narrow)
        grad_hidden = sum(item[1].astype(wide) for item in found)
        if others:
            grad_hidden += zero_of(*others)
        return branch, grad_hidden + dot(logits, router_t, TN), logits

    last_order = list(chunks[1:]) + [0]
    pairs = [chunks[s : s + 2] for s in range(0, tp_count, 2)]
    if split == 2:
        run(1, [0])
        run(1, [1])
    run(0, [0])
    run(0, [1], hidden_pieces[2])
    for which in pairs[1:]:
        if split == 2:
            for s in which:
                run(1, [s])
        run(0, which)
    all_units = jnp.arange(expert_count, dtype=jnp.int32)
    shared_sum = scatter_fsdp(
        grads_of(0, jnp.arange(shared_units, dtype=jnp.int32)).reshape(3 * sff, width), 1
    )
    first_sum = None
    if split == 2:
        first_sum = scatter_fsdp(grads_of(1, all_units).reshape(-1, width))

    pieces, total = {}, None
    for k, s in enumerate(last_order):
        if k == 2:
            previous.append(shared_sum)
            branch_total = after(pieces[last_order[0]][0], *previous)
            previous.append(branch_total)
        if k == tp_count - 1:
            pieces[last_order[1]] = finish_piece(last_order[1], *previous)
            total = (hop(total).astype(wide) + pieces[last_order[1]][1]).astype(narrow)
            branch_total = (
                hop(branch_total).astype(wide) + after(pieces[last_order[1]][0], total)
            ).astype(narrow)
            previous += [total, branch_total]
        run(split, [s])
        if k == 0:
            pieces[s] = finish_piece(s)
            total = pieces[s][1].astype(narrow)
            previous.append(total)
    for s in last_order[2:-1]:
        pieces[s] = finish_piece(s, *previous)
        total = (hop(total).astype(wide) + pieces[s][1]).astype(narrow)
    previous.append(total)
    if first_sum is not None:
        previous.append(first_sum)
    last_sum = scatter_fsdp(grads_of(split, all_units).reshape(-1, width))
    pieces[0] = finish_piece(0, *previous)
    router_gradient = sum(dot(pieces[s][2], hidden_pieces[s], NN) for s in chunks)
    grad_hidden_own = hop(total).astype(wide) + (pieces[0][1] + zero_of(router_gradient))

    hidden_back = jax.vjp(normalize, hidden, ffn_scale)[1]
    grad_hnorm, grad_ffn_gain = hidden_back(grad_hidden_own)
    grad_hidden = grad_out + grad_hnorm
    grad_attn = grad_hidden.astype(narrow)
    branch_total = after(branch_total, grad_attn)
    out_scatter, make_out = scatter_product(grad_attn, mixed)
    grad_mixed = dot(grad_attn, output_whole, NN, narrow)

    def back(first, pairs, rows, latents_before, waits):
        return attend_back(
            query_nope, query_rope, latent_all, kvb_whole, kvb_first, kvb_columns, keyval,
            rows.reshape(seq_count, local_len, -1), log_sums, key_row, limit,
            cosines, sines, latents_before, first, pairs, waits,
        )

    pairs_half = HEAD_COUNT // 4
    first_qn, first_qr, first_latents, first_kvb = back(
        0, pairs_half, grad_mixed, jnp.zeros_like(latent_all), [out_scatter.sent, branch_total]
    )
    first_query = jnp.concatenate([first_qn, first_qr], axis=-1).reshape(own_rows, -1)
    first_scatter, make_first_query = scatter_product(
        normed, first_query, first_kvb.reshape(width, -1)
    )
    out_scatter.join(make_out, first_scatter.sent)
    for s in last_order[2:-1]:
        branch_total = (
            hop(branch_total).astype(wide) + after(pieces[s][0], out_scatter.part)
        ).astype(narrow)
    second_qn, second_qr, grad_latent_all, second_kvb = back(
        pairs_half, pairs_half, grad_mixed, first_latents,
        [branch_total, out_scatter.part, last_sum],
    )

    grad_latent_sum = scatter_tp(grad_latent_all, 1, own_rows)
    second_query = jnp.concatenate([second_qn, second_qr], axis=-1).reshape(own_rows, -1)
    second_scatter, make_second_query = scatter_product(
        normed, second_query, second_kvb.reshape(width, -1)
    )
    out_scatter.turn(second_scatter.sent)
    branch_moved = hop(branch_total)
    first_scatter.join(make_first_query, out_scatter.turned, branch_moved)
    second_scatter.join(make_second_query, first_scatter.part)
    half_plain, half_turned = first_qn.shape[2], first_qr.shape[2]
    query_gradient = jnp.concatenate(
        [
            first_query[:, :half_plain],
            second_query[:, :half_plain],
            first_query[:, half_plain:],
            second_query[:, half_plain:],
        ],
        axis=1,
    )
    grad_normed = dot(after(query_gradient, second_scatter.part), query_whole, NT)
    first_scatter.turn(grad_normed)

    latent_back = jax.vjp(normalize, compressed, latent_scale)[1]
    grad_compressed, grad_latent_gain = latent_back(grad_latent_sum[:, :RANK])
    latent_gradient = jnp.concatenate(
        [
            grad_compressed,
            rotate(grad_latent_sum[:, RANK : RANK + ROTARY_WIDTH], row_positions, -1.0),
        ],
        axis=-1,
    ).astype(narrow)
    latent_key_gradient = dot(latent_gradient, normed, TN)
    grad_normed = grad_normed + dot(latent_gradient, latent_key_whole, NN)
    token_back = jax.vjp(normalize, token_rows, attn_scale)[1]
    grad_tnorm, grad_attn_gain = token_back(grad_normed)
    grad_tokens = (grad_hidden + grad_tnorm).astype(narrow).reshape(tokens.shape)


    small_grads = small_stack(
        latent_key_gradient,
        grad_attn_gain,
        grad_ffn_gain,
        jnp.pad(
            grad_latent_gain.reshape(fsdp_count, latent_shard),
            ((0, 0), (0, shard - latent_shard)),
        ).reshape(-1),
        router_gradient,
    )
    small_sum = cross_sum(scatter_fsdp(small_grads, 1))
    second_scatter.turn(small_grads)

    out_sum = out_scatter.end(small_grads)
    first_own = first_scatter.end()
    second_own = second_scatter.end()
    half_query = half_plain + half_turned

    def query_piece(s):
        half = tp_count // 2
        values, at = (first_own, s) if s < half else (second_own, s - half)
        return jnp.concatenate(
            [
                values[:, at * nope_cols : (at + 1) * nope_cols],
                values[:, half_plain + at * rope_cols : half_plain + (at + 1) * rope_cols],
                values[:, half_query + at * kvb_columns : half_query + (at + 1) * kvb_columns],
            ],
            axis=1,
        )

    out_own = cross_scatter(jnp.split(out_sum, tp_count, axis=1)).T
    query_own = cross_scatter([query_piece(s) for s in chunks])
    branch_own = branch_moved.astype(wide) + after(pieces[0][0], small_grads)
    output = (live_mask * (hidden + branch_own)).astype(narrow).reshape(tokens.shape)
    kvb_own = jnp.concatenate(jnp.split(query_own[:, query_cols:], quarters, axis=0), axis=1)
    query_own = jnp.concatenate(
        [
            query_own[:, :nope_cols].reshape(shard, head_local, PLAIN_WIDTH),
            query_own[:, nope_cols:query_cols].reshape(shard, head_local, ROTARY_WIDTH),
        ],
        axis=-1,
    ).reshape(shard, -1)
    shared_sum = shared_sum.astype(wide).reshape(shared_units, 3, unit, shard)
    expert_sum = [last_sum] if first_sum is None else [first_sum, last_sum]
    expert_sum = jnp.concatenate(
        [item.astype(wide).reshape(3, unit, width) for item in expert_sum], axis=1
    )
    return (
        output,
        grad_tokens,
        small_sum[gain_rows[0]],
        query_own,
        small_sum[:latent_width].T,
        small_sum[gain_rows[2], :latent_shard],
        kvb_own,
        out_own,
        small_sum[gain_rows[1]],
        small_sum[router_first : router_first + expert_count].T,
        shared_sum[:, 0].reshape(sff, shard).T,
        shared_sum[:, 1].reshape(sff, shard).T,
        shared_sum[:, 2].reshape(sff, shard),
        expert_sum[0].T[None],
        expert_sum[1].T[None],
        expert_sum[2][None],
    )


def solution(mesh):
    in_specs = (
        P("fsdp", "tp", None),
        P("fsdp"),
        P("fsdp", None, None),
        P("fsdp", None, None),
        P("fsdp"),
        P("fsdp", "tp"),
        P("fsdp", None),
        P("fsdp"),
        P("fsdp", "tp"),
        P("tp", "fsdp"),
        P("fsdp"),
        P("fsdp", None),
        P("fsdp", "tp"),
        P("fsdp", "tp"),
        P("tp", "fsdp"),
        P("fsdp", None, "tp"),
        P("fsdp", None, "tp"),
        P("fsdp", "tp", None),
        P("fsdp", "tp", None),
    )
    out_specs = (
        P("fsdp", "tp", None),
        P("fsdp", "tp", None),
        P("fsdp"),
        P("fsdp", "tp"),
        P("fsdp", None),
        P("fsdp"),
        P("fsdp", "tp"),
        P("tp", "fsdp"),
        P("fsdp"),
        P("fsdp", None),
        P("fsdp", "tp"),
        P("fsdp", "tp"),
        P("tp", "fsdp"),
        P("fsdp", None, "tp"),
        P("fsdp", None, "tp"),
        P("fsdp", "tp", None),
    )
    return jax.shard_map(
        on_device, mesh=mesh, in_specs=in_specs, out_specs=out_specs, check_vma=False
    )
```
